256 devices in a mesh: sample: 4 (over y), space: 64 (over z, x, core).
Axes of the slice: x: 4, y: 4, z: 8, core: 2. Of those that a mesh axis runs over, the one named last changes fastest.
Arguments:
- volumes: bfloat16 [4, 4, 512, 32, 256], P(None, None, 'space', 'sample'), may hold values from -6 to 6
- weight_one: bfloat16 [16, 4, 3, 3, 3], replicated, may hold values from -0.625 to 0.625
- weight_two: bfloat16 [32, 16, 3, 3, 3], replicated, may hold values from -0.3125 to 0.3125
- weight_three: bfloat16 [64, 32, 3, 3, 3], replicated, may hold values from -0.21875 to 0.21875
- feature_grad: bfloat16 [4, 64, 64, 128], P('sample', None, 'space'), may hold values from -6 to 6
Outputs:
- features: bfloat16 [4, 64, 64, 128], P('sample', None, 'space')
- grad_act_one: bfloat16 [4, 16, 256, 16, 128], P(None, None, 'space', 'sample')
- wgrad_one: float32 [16, 4, 3, 3, 3], replicated
- wgrad_two: float32 [32, 16, 3, 3, 3], replicated
- wgrad_three: float32 [64, 32, 3, 3, 3], replicated
The draws below stay inside these ranges and needn't reach their ends.
All inputs are finite; a program needn't handle non-finite values.
Results may differ from the reference program's by a relative error of at most 0.023.
Values may be sent and summed in bfloat16 or wider, within the bound.
A program may use at most 192 MiB of HBM per device.

```python
import math
import jax
import jax.numpy as jnp
from jax import lax

C0 = 4
C1 = 16
C2 = 32
C3 = 64
NZ = 256
SAMPLES = 4
NX = 512
NY = 32


def shard_levels(rng, dims, split, smallest, high):
    loudness, own = 1.0, jax.random.fold_in(rng, 6)
    for dim, blocks in split:
        steps = jnp.exp(jax.random.uniform(jax.random.fold_in(own, dim), (blocks,), jnp.float32, smallest / len(split), high / len(split)))
        loudness = loudness * jnp.repeat(steps, dims[dim] // blocks).reshape([-1 if axis == dim else 1 for axis in range(len(dims))])
    return loudness


def scatter_about(rng, shape, deviation, bound, shards=(), kind=jnp.bfloat16):
    array = jax.random.normal(rng, shape, jnp.float32) * deviation
    if len(shards) > 0:
        array = shard_levels(rng, shape, shards, -0.22, 0.18) * array
    return jnp.clip(array, min=-bound, max=bound).astype(kind)


def setup_inputs(seed: int = 0) -> dict:
    key_of = jax.random.split(jax.random.key(seed), 6)
    volumes = scatter_about(key_of[0], (SAMPLES, C0, NX, NY, NZ), 1.0, 6.0, ((2, 64), (3, 4)))
    weight_one = scatter_about(key_of[1], (C1, C0, 3, 3, 3), (C0 * 27) ** -0.5, 0.625)
    weight_two = scatter_about(key_of[2], (C2, C1, 3, 3, 3), (C1 * 27) ** -0.5, 0.3125)
    weight_three = scatter_about(key_of[3], (C3, C2, 3, 3, 3), (C2 * 27) ** -0.5, 0.21875)
    feature_grad = scatter_about(key_of[4], (SAMPLES, C3, NX // 8, (NY // 8) * (NZ // 8)), 1.0, 6.0, ((0, 4), (2, 64)))
    return {"volumes": volumes, "weight_one": weight_one, "weight_two": weight_two, "weight_three": weight_three, "feature_grad": feature_grad}


LAYOUT = ('NCDHW', 'OIDHW', 'NCDHW')
GRAD_GAIN = 4.0

def strided_conv(inputs, weights):
    return lax.conv_general_dilated(inputs, weights, (2, 2, 2), ((0, 1), (0, 1), (0, 1)), dimension_numbers=LAYOUT, precision=lax.Precision.HIGHEST)

def activate(pre_act):
    root = jnp.sqrt(pre_act * pre_act + 1.0)
    active = (0.65 * pre_act + 0.35 * (root - 1.0)).astype(jnp.bfloat16)
    slope = (0.65 + 0.35 * pre_act / root).astype(jnp.bfloat16)
    return lax.optimization_barrier((active, slope))

def reference(volumes, weight_one, weight_two, weight_three, feature_grad):
    filter_one = weight_one.astype(jnp.float32)
    filter_two = weight_two.astype(jnp.float32)
    filter_three = weight_three.astype(jnp.float32)

    def one_sample(sample_pair):
        volume, cotangent = sample_pair
        inputs = volume[None].astype(jnp.float32)
        pre_one, back_one = jax.vjp(lambda kernel: strided_conv(inputs, kernel), filter_one)
        act_one, slope_one = activate(pre_one)
        pre_two, back_two = jax.vjp(strided_conv, act_one.astype(jnp.float32), filter_two)
        act_two, slope_two = activate(pre_two)
        pre_three, back_three = jax.vjp(strided_conv, act_two.astype(jnp.float32), filter_three)
        act_three, slope_three = activate(pre_three)
        grad_three = lax.optimization_barrier((cotangent.reshape(pre_three.shape).astype(jnp.float32) * slope_three.astype(jnp.float32)).astype(jnp.bfloat16))
        down_two, wgrad_three = back_three(grad_three.astype(jnp.float32))
        down_two = lax.optimization_barrier(down_two.astype(jnp.bfloat16))
        grad_two = lax.optimization_barrier((down_two.astype(jnp.float32) * slope_two.astype(jnp.float32)).astype(jnp.bfloat16))
        down_one, wgrad_two = back_two(grad_two.astype(jnp.float32))
        grad_one = lax.optimization_barrier((down_one * slope_one.astype(jnp.float32)).astype(jnp.bfloat16))
        wgrad_one = back_one(grad_one.astype(jnp.float32))[0]
        return (act_three.reshape(cotangent.shape), down_one[0].astype(jnp.bfloat16), wgrad_one, wgrad_two, wgrad_three)
    results = lax.map(one_sample, (volumes, feature_grad))
    scale_one = GRAD_GAIN / math.sqrt(SAMPLES * (NX // 2) * (NY // 2) * (NZ // 2))
    scale_two = GRAD_GAIN / math.sqrt(SAMPLES * (NX // 4) * (NY // 4) * (NZ // 4))
    scale_three = GRAD_GAIN / math.sqrt(SAMPLES * (NX // 8) * (NY // 8) * (NZ // 8))
    wgrad_one = lax.optimization_barrier(jnp.sum(results[2], axis=0)) * scale_one
    wgrad_two = lax.optimization_barrier(jnp.sum(results[3], axis=0)) * scale_two
    wgrad_three = lax.optimization_barrier(jnp.sum(results[4], axis=0)) * scale_three
    return (results[0], results[1], wgrad_one, wgrad_two, wgrad_three)
```

```python
import math

import jax
import jax.numpy as jnp
import ml_dtypes
import numpy as np
from jax import lax
from jax.experimental import pallas as pl
from jax.experimental.pallas import tpu as pltpu
from jax.sharding import PartitionSpec as P

GRAD_GAIN = 4.0
MESH = pl.DeviceIdType.MESH
F32 = jnp.float32
BF16 = jnp.bfloat16
TAPS_THREE = {-1: (1, 2), 0: (0, 1)}
TAPS_TWO = {-1: (2,), 0: (0, 1, 2), 1: (0, 1)}
COPIES = 128


def every_second(blocks, cells):
    half = cells // 2
    out = np.zeros((blocks, cells, 3, blocks, half), np.float32)
    for b in range(blocks):
        for f in range(3):
            for k in range(half):
                if 2 * k + f < cells:
                    out[b, 2 * k + f, f, b, k] = 1
    return out.reshape(blocks * cells, 3 * blocks * half)


def row_orders():
    main = np.zeros((8, 8, 16, 3, 4, 8, 8), np.float32)
    halo = np.zeros((17, 16, 3, 80), np.float32)
    edge = np.zeros((80, 4, 8, 8), np.float32)
    pads = np.zeros((9, 16, 9, 12), np.float32)
    cells = np.zeros((16, 4, 4, 4, 4, 16), np.float32)
    for c in range(4):
        for x in range(8):
            for y in range(8):
                for f in range(3):
                    main[x, y, f * 4 + c, f, c, x, y] = 1
        for u in range(8):
            edge[c * 8 + u, c, 0, u] = 1
            edge[32 + c * 8 + u, c, u, 0] = 1
            for f in range(3):
                halo[u, f * 4 + c, f, c * 8 + u] = 1
                halo[9 + u, f * 4 + c, f, 32 + c * 8 + u] = 1
        edge[64 + c, c, 0, 0] = 1
        for f in range(3):
            halo[8, f * 4 + c, f, 64 + c] = 1
    for t in range(9):
        for r in range(12):
            pads[t, r, t, r] = 1
    for c in range(16):
        for x in range(4):
            for y in range(4):
                cells[c, x, y, x, y, c] = 1
    return (
        main.reshape(1024, 768),
        halo.reshape(272, 240),
        edge.reshape(80, 256),
        pads.reshape(144, 108),
        cells.reshape(256, 256),
    )


def mm(a, b):
    return jnp.dot(a, b, preferred_element_type=F32)


def mm_t(a, b):
    return lax.dot_general(a, b, (((1,), (1,)), ((), ())), preferred_element_type=F32)


def activate(p):
    square = p * p + 1.0
    inverse = lax.rsqrt(square)
    active = (0.65 * p + 0.35 * (square * inverse - 1.0)).astype(BF16)
    slope = (0.65 + 0.35 * (p * inverse)).astype(BF16)
    return active, slope


def identity(n):
    return (
        lax.broadcasted_iota(jnp.int32, (n, n), 0) == lax.broadcasted_iota(jnp.int32, (n, n), 1)
    ).astype(F32).astype(BF16)


def make_kernel(ny, ns, gx, scales):
    gz = ns // gx
    rows3 = 128 // gx

    def kernel(vol, w1t, w2t, w3t, fg, s1, s2, s3, pm, ph, pq, pw, po, feat, gact, o1, o2, o3,
               w1, w2, w3, w2k, w3k, hs, hr, vsm, vsh, e1, a1, sl1, e2, a2, sl2, e3, fgs, fts,
               g3, gg3, g2e, gg2, d1b, wb3, r3, p3, q3, z3, f3, wb2, y2, p2, q2, z2, f2,
               y1, x1, z1, ss, rs):
        y = lax.axis_index("sample")
        s = lax.axis_index("space")
        gx_me = lax.rem(s, gx)
        gz_me = lax.div(s, gx)
        y_prev, y_next = lax.rem(y + ny - 1, ny), lax.rem(y + 1, ny)
        s_prev, s_next = lax.rem(s + ns - 1, ns), lax.rem(s + 1, ns)
        y_peers = [{"sample": lax.rem(y + d, ny), "space": s} for d in range(1, ny)]
        x_peers = [{"sample": y, "space": gz_me * gx + lax.rem(gx_me + d, gx)} for d in range(1, gx)]
        z_peers = [{"sample": y, "space": lax.rem(s + d * gx, ns)} for d in range(1, gz)]
        prev = [
            {"sample": y, "space": s_prev},
            {"sample": y_prev, "space": s},
            {"sample": y_prev, "space": s_prev},
        ]
        following = [
            {"sample": y, "space": s_next},
            {"sample": y_next, "space": s},
            {"sample": y_next, "space": s_next},
        ]
        started = []

        def send(src, dst, device):
            n = len(started)
            copy = pltpu.make_async_remote_copy(
                src_ref=src, dst_ref=dst, send_sem=ss.at[n], recv_sem=rs.at[n],
                device_id=device, device_id_type=MESH,
            )
            copy.start()
            started.append(copy)
            return copy

        def arrive(copies):
            for copy in copies:
                copy.wait_recv()

        barrier = pltpu.get_barrier_semaphore()
        greeted = y_peers + x_peers + z_peers + [prev[0], prev[2], following[0], following[2]]
        for device in greeted:
            pl.semaphore_signal(barrier, inc=1, device_id=device, device_id_type=MESH)

        more_x = jnp.where(s == ns - 1, 0.0, 1.0).astype(F32)
        more_y = jnp.where(y == ny - 1, 0.0, 1.0).astype(F32)
        less_x = jnp.where(s == 0, 0.0, 1.0).astype(F32)
        less_y = jnp.where(y == 0, 0.0, 1.0).astype(F32)

        for b in range(4):
            hs[b] = mm(pq[...], vol[b]).astype(BF16)
        fgs[y] = fg[...]
        pl.semaphore_wait(barrier, len(greeted))
        spans = ((0, 32), (32, 32), (64, 16))
        got_vol = [
            send(hs.at[:, pl.ds(at, n)], hr.at[:, pl.ds(at, n)], prev[i])
            for i, (at, n) in enumerate(spans)
        ]
        got_fg = [send(fgs.at[y], fgs.at[y], device) for device in y_peers]

        w1pad = mm(pw[...], w1t[...]).astype(BF16)
        w1[...] = mm_t(identity(16), w1pad).astype(BF16)
        w2[...] = mm_t(identity(32), w2t[...]).astype(BF16)
        w3[...] = mm_t(identity(64), w3t[...]).astype(BF16)
        w2rows = w2t[...].reshape(9, 3, 16, 32)
        w3rows = w3t[...].reshape(9, 3, 32, 64)
        for f in range(3):
            w2k[:, f * 32:(f + 1) * 32] = w2rows[:, f].reshape(144, 32)
            w3k[:, f * 64:(f + 1) * 64] = w3rows[:, f].reshape(288, 64)

        for b in range(4):
            part = mm(vol[b], s1[...]).astype(BF16)
            for f in range(3):
                vsm[f * 256:(f + 1) * 256, b * 128:(b + 1) * 128] = part[:, f * 128:(f + 1) * 128]
        for x in range(8):
            block = mm(pm[x * 128:(x + 1) * 128, :], vsm[...]).astype(BF16)
            e1[x * 9:x * 9 + 8] = block.reshape(8, 16, 512)

        arrive(got_vol)
        row = lax.broadcasted_iota(jnp.int32, (80, 384), 0)
        inside = jnp.where(row < 32, more_x, jnp.where(row < 64, more_y, more_x * more_y))
        for b in range(4):
            part = (mm(hr[b], s1[...]) * inside).astype(BF16)
            for f in range(3):
                vsh[f * 80:(f + 1) * 80, b * 128:(b + 1) * 128] = part[:, f * 128:(f + 1) * 128]
        block = mm(ph[...], vsh[...]).astype(BF16).reshape(17, 16, 512)
        e1[72:81] = block[:9]
        for x in range(8):
            e1[x * 9 + 8] = block[9 + x]

        def columns_one(i, j):
            return jnp.concatenate(
                [e1[(2 * i + a) * 9 + 2 * j:(2 * i + a) * 9 + 2 * j + 3].reshape(48, 512) for a in range(3)],
                axis=0,
            )

        def cell_one(i, j):
            act, slope = activate(mm(w1[...], columns_one(i, j)))
            a1[i * 5 + j] = act
            sl1[i * 4 + j] = slope

        for j in range(4):
            cell_one(0, j)
        got_act = [
            send(a1.at[pl.ds(0, 4)], a1.at[pl.ds(20, 4)], prev[0]),
            send(a1.at[0], a1.at[24], prev[2]),
        ]
        got_rows = [send(a1.at[0], a1.at[4], prev[1])]
        for i in range(1, 4):
            for j in range(4):
                cell_one(i, j)
                if j == 0:
                    got_rows.append(send(a1.at[i * 5], a1.at[i * 5 + 4], prev[1]))

        def widen_two(cells, rows, keep):
            for p in range(2):
                part = mm(rows[:, p * 256:(p + 1) * 256], s2[...])
                if keep is not None:
                    part = part * keep
                part = part.astype(BF16).reshape(len(cells), 16, 384)
                for n, cell in enumerate(cells):
                    for f in range(3):
                        e2[cell, f * 16:(f + 1) * 16, p * 128:(p + 1) * 128] = part[n, :, f * 128:(f + 1) * 128]

        for x in range(4):
            widen_two([x * 5 + k for k in range(4)], a1[x * 5:x * 5 + 4].reshape(64, 512), None)
        arrive(got_act + got_rows)
        far = [20, 21, 22, 23, 24, 4, 9, 14, 19]
        row = lax.broadcasted_iota(jnp.int32, (144, 384), 0)
        inside = jnp.where(row < 64, more_x, jnp.where(row < 80, more_x * more_y, more_y))
        widen_two(far, jnp.concatenate([a1[cell] for cell in far], axis=0), inside)

        def columns_two(i, j):
            return jnp.concatenate(
                [e2[(2 * i + a) * 5 + 2 * j:(2 * i + a) * 5 + 2 * j + 3].reshape(144, 256) for a in range(3)],
                axis=0,
            )

        for i in range(2):
            for j in range(2):
                act, slope = activate(mm(w2[...], columns_two(i, j)))
                a2[i * 3 + j] = act
                sl2[(i + 1) * 3 + j + 1] = slope
        got_act = [
            send(a2.at[pl.ds(0, 2)], a2.at[pl.ds(6, 2)], prev[0]),
            send(a2.at[0], a2.at[2], prev[1]),
            send(a2.at[3], a2.at[5], prev[1]),
            send(a2.at[0], a2.at[8], prev[2]),
        ]
        got_slope = [
            send(sl2.at[pl.ds(7, 2)], sl2.at[pl.ds(1, 2)], following[0]),
            send(sl2.at[5], sl2.at[3], following[1]),
            send(sl2.at[8], sl2.at[6], following[1]),
            send(sl2.at[8], sl2.at[0], following[2]),
        ]

        def widen_three(cells, rows, keep):
            part = mm(rows, s3[...])
            if keep is not None:
                part = part * keep
            part = part.astype(BF16).reshape(len(cells), 32, 384)
            for n, cell in enumerate(cells):
                for f in range(3):
                    e3[cell, f * 32:(f + 1) * 32, :] = part[n, :, f * 128:(f + 1) * 128]

        near = [0, 1, 3, 4]
        widen_three(near, jnp.concatenate([a2[cell] for cell in near], axis=0), None)
        row = lax.broadcasted_iota(jnp.int32, (512, 128), 0)
        lane = lax.broadcasted_iota(jnp.int32, (512, 128), 1)
        source = lax.div(lane, 32) * 128 + y * 32 + lax.rem(lane, 32)
        regroup = (row == source).astype(F32).astype(BF16)
        arrive(got_fg)
        cotangent = mm(jnp.concatenate([fgs[k] for k in range(4)], axis=1), regroup)
        arrive(got_act)
        far = [6, 7, 8, 2, 5]
        row = lax.broadcasted_iota(jnp.int32, (160, 384), 0)
        inside = jnp.where(row < 64, more_x, jnp.where(row < 96, more_x * more_y, more_y))
        widen_three(far, jnp.concatenate([a2[cell] for cell in far], axis=0), inside)
        act, slope = activate(mm(w3[...], e3[...].reshape(864, 128)))
        grad_three = (cotangent * slope.astype(F32)).astype(BF16)
        g3[3] = grad_three
        fts[y] = act
        got_grad = [send(g3.at[3], g3.at[to], following[i]) for i, to in enumerate((1, 2, 0))]
        got_feat = [send(fts.at[y], fts.at[y], device) for device in y_peers]

        part = mm_t(e3[...].reshape(864, 128), grad_three)
        wb3[...] = jnp.zeros_like(wb3)
        for n in range(27):
            group, at = divmod(n * 16, rows3)
            for half in range(2):
                wb3[group // gx, group % gx, at:at + 16, half * 64:(half + 1) * 64] = (
                    part[half * 432 + n * 16:half * 432 + (n + 1) * 16]
                )
        got_r3 = [
            send(wb3.at[device["sample"]], r3.at[d], device) for d, device in enumerate(y_peers)
        ]

        arrive(got_grad)
        row = lax.broadcasted_iota(jnp.int32, (256, 128), 0)
        inside = jnp.where(
            row < 64, less_x * less_y, jnp.where(row < 128, less_x, jnp.where(row < 192, less_y, 1.0))
        )
        rows = (g3[...].reshape(256, 128).astype(F32) * inside).astype(BF16)
        for f in range(3):
            part = mm_t(rows, s3[:, f * 128:(f + 1) * 128]).astype(BF16)
            gg3[:, f * 64:(f + 1) * 64, :] = part.reshape(4, 64, 256)
        down = {}
        for i in (-1, 0):
            for j in (-1, 0):
                picked = jnp.concatenate(
                    [w3k[(a * 3 + e) * 32:(a * 3 + e + 1) * 32, :] for a in TAPS_THREE[i] for e in TAPS_THREE[j]],
                    axis=0,
                )
                part = mm(picked, gg3[(i + 1) * 2 + j + 1])
                n = 0
                for a in TAPS_THREE[i]:
                    for e in TAPS_THREE[j]:
                        key = (2 * i + a, 2 * j + e)
                        term = part[n * 32:(n + 1) * 32]
                        down[key] = term if key not in down else down[key] + term
                        n += 1
        arrive(got_slope)
        for i in range(-1, 2):
            for j in range(-1, 2):
                cell = (i + 1) * 3 + j + 1
                rounded = down[i, j].astype(BF16).astype(F32)
                g2e[cell] = (rounded * sl2[cell].astype(F32)).astype(BF16)

        part = None
        for i in range(2):
            for j in range(2):
                term = mm_t(columns_two(i, j), g2e[(i + 1) * 3 + j + 1])
                part = term if part is None else part + term
        wb2[...] = jnp.zeros_like(wb2)
        for n in range(27):
            lanes, at = divmod(n * 16, 112)
            wb2[at:at + 16, lanes * 32:(lanes + 1) * 32] = part[n * 16:(n + 1) * 16]
        y2[y] = wb2[...]
        got_y2 = [send(y2.at[y], y2.at[y], device) for device in y_peers]

        arrive(got_r3)
        p3[...] = (wb3[y] + r3[0]) + (r3[1] + r3[2])
        got_q3 = [
            send(p3.at[lax.rem(gx_me + d + 1, gx)], q3.at[d], device) for d, device in enumerate(x_peers)
        ]

        for p in range(2):
            rows = g2e[...].reshape(288, 256)[:, p * 128:(p + 1) * 128]
            for f in range(3):
                part = mm_t(rows, s2[:, f * 128:(f + 1) * 128]).astype(BF16)
                gg2[:, f * 32:(f + 1) * 32, p * 256:(p + 1) * 256] = part.reshape(9, 32, 256)
        down = {}
        for i in (-1, 0, 1):
            for j in (-1, 0, 1):
                picked = jnp.concatenate(
                    [w2k[(a * 3 + e) * 16:(a * 3 + e + 1) * 16, :] for a in TAPS_TWO[i] for e in TAPS_TWO[j]],
                    axis=0,
                )
                part = mm(picked, gg2[(i + 1) * 3 + j + 1])
                n = 0
                for a in TAPS_TWO[i]:
                    for e in TAPS_TWO[j]:
                        key = (2 * i + a, 2 * j + e)
                        term = part[n * 16:(n + 1) * 16]
                        down[key] = term if key not in down else down[key] + term
                        n += 1

        part = None
        for i in range(4):
            for j in range(4):
                d1b[(i * 4 + j) * 16:(i * 4 + j + 1) * 16, :] = down[i, j].astype(BF16)
                grad_one = (down[i, j] * sl1[i * 4 + j].astype(F32)).astype(BF16)
                term = mm_t(columns_one(i, j), grad_one)
                part = term if part is None else part + term
        y1[y, :, 0:144] = part.T
        y1[y, :, 144:256] = jnp.zeros((16, 112), F32)
        got_y1 = [send(y1.at[y], y1.at[y], device) for device in y_peers]

        arrive(got_y2)
        total = (y2[0] + y2[1]) + (y2[2] + y2[3])
        for t in range(gx):
            p2[t] = total[t * rows3:(t + 1) * rows3]
        got_q2 = [
            send(p2.at[lax.rem(gx_me + d + 1, gx)], q2.at[d], device) for d, device in enumerate(x_peers)
        ]
        arrive(got_q3)
        total = p3[gx_me]
        for d in range(gx - 1):
            total = total + q3[d]
        z3[gz_me] = total
        got_z3 = [send(z3.at[gz_me], z3.at[gz_me], device) for device in z_peers]

        block = mm(po[...], d1b[...]).astype(BF16)
        for b in range(4):
            gact[b] = block[:, b * 128:(b + 1) * 128]
        arrive(got_feat)
        feat[...] = mm(jnp.concatenate([fts[k] for k in range(4)], axis=1), regroup).astype(BF16)

        arrive(got_y1)
        x1[gx_me] = (y1[0] + y1[1]) + (y1[2] + y1[3])
        got_x1 = [send(x1.at[gx_me], x1.at[gx_me], device) for device in x_peers]
        arrive(got_q2)
        total = p2[gx_me]
        for d in range(gx - 1):
            total = total + q2[d]
        z2[gz_me] = total
        got_z2 = [send(z2.at[gz_me], z2.at[gz_me], device) for device in z_peers]
        arrive(got_z3)
        total = z3[0]
        for d in range(1, gz):
            total = total + z3[d]
        f3[y, gx_me] = total * scales[2]
        got_f3 = [send(f3.at[y, gx_me], f3.at[y, gx_me], device) for device in x_peers]

        arrive(got_x1)
        total = x1[0]
        for d in range(1, gx):
            total = total + x1[d]
        z1[gz_me] = total
        got_z1 = [send(z1.at[gz_me], z1.at[gz_me], device) for device in z_peers]
        arrive(got_z2)
        total = z2[0]
        for d in range(1, gz):
            total = total + z2[d]
        f2[gx_me] = total * scales[1]
        got_f2 = [send(f2.at[gx_me], f2.at[gx_me], device) for device in x_peers]
        arrive(got_f3)
        got_last = [send(f3.at[y], f3.at[y], device) for device in y_peers]

        arrive(got_z1)
        total = z1[0]
        for d in range(1, gz):
            total = total + z1[d]
        total = (total * scales[0]).T
        for t in range(9):
            o1[t * 12:(t + 1) * 12, :] = total[t * 16:t * 16 + 12]
        arrive(got_f2)
        total = f2[...].reshape(128, 128)
        for n in range(27):
            lanes, at = divmod(n * 16, 112)
            o2[n * 16:(n + 1) * 16, :] = total[at:at + 16, lanes * 32:(lanes + 1) * 32]
        arrive(got_last)
        total = f3[...].reshape(512, 128)[:432]
        for half in range(2):
            o3[half * 432:(half + 1) * 432, :] = total[:, half * 64:(half + 1) * 64]
        for copy in started:
            copy.wait_send()

    vm = pltpu.VMEM
    scratch = [
        vm((16, 144), BF16), vm((32, 432), BF16), vm((64, 864), BF16), vm((144, 96), BF16), vm((288, 192), BF16),
        vm((4, 80, 256), BF16), vm((4, 80, 256), BF16), vm((768, 512), BF16), vm((240, 512), BF16),
        vm((81, 16, 512), BF16), vm((25, 16, 512), BF16), vm((16, 16, 512), BF16), vm((25, 48, 256), BF16),
        vm((9, 32, 256), BF16), vm((9, 32, 256), BF16), vm((9, 96, 128), BF16),
        vm((4, 64, 128), BF16), vm((4, 64, 128), BF16), vm((4, 64, 128), BF16), vm((4, 192, 256), BF16),
        vm((9, 32, 256), BF16), vm((9, 96, 512), BF16), vm((256, 512), BF16),
        vm((ny, gx, rows3, 128), F32), vm((ny - 1, gx, rows3, 128), F32), vm((gx, rows3, 128), F32),
        vm((gx - 1, rows3, 128), F32), vm((gz, rows3, 128), F32), vm((ny, gx, rows3, 128), F32),
        vm((128, 128), F32), vm((ny, 128, 128), F32), vm((gx, rows3, 128), F32), vm((gx - 1, rows3, 128), F32),
        vm((gz, rows3, 128), F32), vm((gx, rows3, 128), F32),
        vm((ny, 16, 256), F32), vm((gx, 16, 256), F32), vm((gz, 16, 256), F32),
        pltpu.SemaphoreType.DMA((COPIES,)), pltpu.SemaphoreType.DMA((COPIES,)),
    ]
    return pl.pallas_call(
        kernel,
        out_shape=(
            jax.ShapeDtypeStruct((64, 128), BF16),
            jax.ShapeDtypeStruct((4, 256, 128), BF16),
            jax.ShapeDtypeStruct((108, 16), F32),
            jax.ShapeDtypeStruct((432, 32), F32),
            jax.ShapeDtypeStruct((864, 64), F32),
        ),
        in_specs=[pl.BlockSpec(memory_space=pltpu.VMEM)] * 13,
        out_specs=[pl.BlockSpec(memory_space=pltpu.VMEM)] * 5,
        scratch_shapes=scratch,
        compiler_params=pltpu.CompilerParams(
            collective_id=0, has_side_effects=True, vmem_limit_bytes=48 * 1024 * 1024
        ),
        cost_estimate=pl.CostEstimate(flops=6_000_000_000, bytes_accessed=8_000_000, transcendentals=0),
        name="layers",
    )


def solution(mesh):
    ny, ns = mesh.shape["sample"], mesh.shape["space"]
    gx = 8 if ns % 8 == 0 and ns > 8 else 2
    select = [every_second(1, 256), every_second(2, 128), every_second(4, 64)]
    consts = [np.asarray(c).astype(ml_dtypes.bfloat16) for c in select + list(row_orders())]

    def local(volumes, weight_one, weight_two, weight_three, feature_grad):
        cells = volumes.shape[0] * volumes.shape[2] * ns * volumes.shape[3] * ny * volumes.shape[4]
        scales = [GRAD_GAIN / math.sqrt(cells // 8**n) for n in (1, 2, 3)]
        flat = [
            jnp.transpose(w, (2, 3, 4, 1, 0)).reshape(-1, w.shape[0])
            for w in (weight_one, weight_two, weight_three)
        ]
        features, grad_act, one, two, three = make_kernel(ny, ns, gx, scales)(
            volumes.reshape(4, 256, 256), *flat, feature_grad.reshape(64, 128), *consts
        )

        def filters(array, channels):
            return jnp.transpose(array.reshape(3, 3, 3, channels, -1), (4, 3, 0, 1, 2))

        return (
            features.reshape(feature_grad.shape),
            grad_act.reshape(4, 16, 4, 4, 128),
            filters(one, 4),
            filters(two, 16),
            filters(three, 32),
        )

    in_specs = (
        P(None, None, "space", "sample", None),
        P(),
        P(),
        P(),
        P("sample", None, "space", None),
    )
    out_specs = (
        P("sample", None, "space", None),
        P(None, None, "space", "sample", None),
        P(),
        P(),
        P(),
    )
    return jax.shard_map(local, mesh=mesh, in_specs=in_specs, out_specs=out_specs, check_vma=False)
```

```python
import math

import jax
import jax.numpy as jnp
from jax import lax
from jax.experimental import pallas as pl
from jax.experimental.pallas import tpu as pltpu
from jax.sharding import PartitionSpec as P

GRAD_GAIN = 4.0
MESH = pl.DeviceIdType.MESH
F32 = jnp.float32
BF16 = jnp.bfloat16
TAPS_THREE = {-1: (1, 2), 0: (0, 1)}
TAPS_TWO = {-1: (2,), 0: (0, 1, 2), 1: (0, 1)}
COPIES = 192


def mm(a, b):
    return jnp.dot(a, b, preferred_element_type=F32)


def mm_t(a, b):
    return lax.dot_general(a, b, (((1,), (1,)), ((), ())), preferred_element_type=F32)


def activate(p):
    square = p * p + 1.0
    inverse = lax.rsqrt(square)
    active = (0.65 * p + 0.35 * (square * inverse - 1.0)).astype(BF16)
    slope = (0.65 + 0.35 * (p * inverse)).astype(BF16)
    return active, slope


def identity(n):
    return (
        lax.broadcasted_iota(jnp.int32, (n, n), 0) == lax.broadcasted_iota(jnp.int32, (n, n), 1)
    ).astype(F32).astype(BF16)


def grid(rows, lanes):
    return (
        lax.broadcasted_iota(jnp.int32, (rows, lanes), 0),
        lax.broadcasted_iota(jnp.int32, (rows, lanes), 1),
    )


def marks(condition):
    return condition.astype(F32).astype(BF16)


def make_kernel(ny, ns, nx, scales):
    n_near, n_far = ny * nx, ns // nx
    rows3, rows2 = 512 // n_near, 128 // n_near

    def kernel(vol_in, w1t_in, w2t_in, w3t_in, fg_in, feat_out, gact_out, o1_out, o2_out, o3_out,
               vol, w1t, w2t, w3t, fg, ls, feat, gact, o1, o2, o3, os,
               s1, s2, s3, pm, w1, w2, w3, w2k, w3k, hs, hr, vsm, e1, a1, sl1, e2, a2, sl2, e3, fgs, fts,
               g3, gg3, g2e, gg2, d1b, wb3, r3, z3, f3, wb2, r2, z2, f2, y1, z1, ss, rs):
        y = lax.axis_index("sample")
        s = lax.axis_index("space")
        z_me = lax.div(s, 2 * nx)
        x_me = lax.div(lax.rem(s, 2 * nx), 2)
        core = lax.rem(s, 2)
        near_me = y * nx + x_me
        far_me = z_me * 2 + core
        near_ids = [lax.rem(near_me + d, n_near) for d in range(1, n_near)]
        far_ids = [lax.rem(far_me + d, n_far) for d in range(1, n_far)]
        near = [
            {"sample": lax.div(m, nx), "space": z_me * 2 * nx + lax.rem(m, nx) * 2 + core} for m in near_ids
        ]
        far = [
            {"sample": y, "space": lax.div(m, 2) * 2 * nx + x_me * 2 + lax.rem(m, 2)} for m in far_ids
        ]
        y_peers = [{"sample": lax.rem(y + d, ny), "space": s} for d in range(1, ny)]
        y_prev, y_next = lax.rem(y + ny - 1, ny), lax.rem(y + 1, ny)
        s_prev, s_next = lax.rem(s + ns - 1, ns), lax.rem(s + 1, ns)
        prev = [
            {"sample": y, "space": s_prev},
            {"sample": y_prev, "space": s},
            {"sample": y_prev, "space": s_prev},
        ]
        following = [
            {"sample": y, "space": s_next},
            {"sample": y_next, "space": s},
            {"sample": y_next, "space": s_next},
        ]
        started = []
        stores = []

        def send(src, dst, device):
            n = len(started)
            copy = pltpu.make_async_remote_copy(
                src_ref=src, dst_ref=dst, send_sem=ss.at[n], recv_sem=rs.at[n],
                device_id=device, device_id_type=MESH,
            )
            copy.start()
            started.append(copy)
            return copy

        def arrive(*copies):
            for copy in copies:
                copy.wait_recv()

        def store(src, dst):
            copy = pltpu.make_async_copy(src, dst, os.at[len(stores)])
            copy.start()
            stores.append(copy)

        barrier = pltpu.get_barrier_semaphore()
        greeted = [prev[0], following[0], prev[2], following[2]] + near + far
        for device in greeted:
            pl.semaphore_signal(barrier, inc=1, device_id=device, device_id_type=MESH)

        loads = {}
        for n, (name, src, dst) in enumerate((
            ("vol", vol_in, vol), ("fg", fg_in, fg), ("w1t", w1t_in, w1t), ("w2t", w2t_in, w2t), ("w3t", w3t_in, w3t),
        )):
            loads[name] = pltpu.make_async_copy(src, dst, ls.at[n])
            loads[name].start()

        def loaded(*names):
            for name in names:
                loads.pop(name).wait()

        more_x = jnp.where(s == ns - 1, 0.0, 1.0).astype(F32)
        more_y = jnp.where(y == ny - 1, 0.0, 1.0).astype(F32)
        less_x = jnp.where(s == 0, 0.0, 1.0).astype(F32)
        less_y = jnp.where(y == 0, 0.0, 1.0).astype(F32)
        more_xy = more_x * more_y

        row, lane = grid(80, 256)
        edge = marks(
            ((row < 32) & (lane == (row >> 3) * 64 + (row & 7)))
            | ((row >= 32) & (row < 64) & (lane == (row - 32) * 8))
            | ((row >= 64) & (row < 68) & (lane == (row - 64) * 64))
        )
        for ref, last in ((s1, 127), (s2, 63), (s3, 31)):
            row, lane = grid(256, 128)
            for f in range(3):
                hit = row == 2 * lane + f
                if f == 2:
                    hit = hit & ((lane & last) != last)
                ref[:, f * 128:(f + 1) * 128] = marks(hit)
        row, lane = grid(128, 96)
        pm[...] = marks(((row & 15) == (lane >> 3)) & ((row >> 4) == (lane & 7)))

        loaded("vol", "fg")
        for b in range(4):
            hs[b] = mm(edge, vol[b]).astype(BF16)
        fgs[y] = fg[...]
        pl.semaphore_wait(barrier, len(greeted))
        vol_row = send(hs.at[:, pl.ds(32, 32)], hr.at[:, pl.ds(32, 32)], prev[1])
        vol_plane = send(hs.at[:, pl.ds(0, 32)], hr.at[:, pl.ds(0, 32)], prev[0])
        vol_corner = send(hs.at[:, pl.ds(64, 16)], hr.at[:, pl.ds(64, 16)], prev[2])

        for b in range(4):
            part = mm(vol[b], s1[...]).reshape(4, 8, 8, 384)
            for x in range(8):
                rows = part[:, x].reshape(32, 384)
                rows = jnp.concatenate([rows[:, f * 128:(f + 1) * 128] for f in range(3)], axis=0)
                vsm[x, :, b * 128:(b + 1) * 128] = rows.astype(BF16)
        for x in range(8):
            e1[x, 0:8] = mm(pm[...], vsm[x]).astype(BF16).reshape(8, 16, 512)
        loaded("w1t", "w2t", "w3t")
        row, lane = grid(144, 108)
        pads = marks((lane == (row >> 4) * 12 + (row & 15)) & ((row & 15) < 12))
        w1rows = w1t[...].astype(F32).reshape(108, 16).astype(BF16)
        w1[...] = mm_t(identity(16), mm(pads, w1rows).astype(BF16)).astype(BF16)
        w2[...] = mm_t(identity(32), w2t[...]).astype(BF16)

        def columns_one(i, j):
            return jnp.concatenate(
                [e1[2 * i + a, 2 * j:2 * j + 3].reshape(48, 512) for a in range(3)], axis=0
            )

        def cell_one(i, j):
            act, slope = activate(mm(w1[...], columns_one(i, j)))
            a1[i, j] = act
            sl1[i * 4 + j] = slope

        def widen_two(cells, keep=None):
            rows = jnp.concatenate([a1[i, j] for i, j in cells], axis=0)
            rows = jnp.concatenate([rows[:, :256], rows[:, 256:]], axis=0)
            part = mm(rows, s2[...])
            if keep is not None:
                part = part * keep
            part = part.astype(BF16).reshape(2, len(cells), 16, 384)
            for p in range(2):
                for n, (i, j) in enumerate(cells):
                    for f in range(3):
                        e2[i, j, f * 16:(f + 1) * 16, p * 128:(p + 1) * 128] = (
                            part[p, n, :, f * 128:(f + 1) * 128]
                        )

        def columns_two(i, j):
            return jnp.concatenate(
                [e2[2 * i + a, 2 * j:2 * j + 3].reshape(144, 256) for a in range(3)], axis=0
            )

        def cell_two(i, j):
            act, slope = activate(mm(w2[...], columns_two(i, j)))
            a2[i, j] = act
            sl2[i + 1, j + 1] = slope

        def widen_three(cells, keep=None):
            part = mm(jnp.concatenate([a2[i, j] for i, j in cells], axis=0), s3[...])
            if keep is not None:
                part = part * keep
            part = part.astype(BF16).reshape(len(cells), 32, 384)
            for n, (i, j) in enumerate(cells):
                for f in range(3):
                    e3[i, j, f * 32:(f + 1) * 32, :] = part[n, :, f * 128:(f + 1) * 128]

        for i in range(3):
            cell_one(i, 0)
        act_row = send(a1.at[pl.ds(0, 3), 0], a1.at[pl.ds(0, 3), 4], prev[1])
        for j in range(1, 3):
            cell_one(0, j)
        act_plane = send(a1.at[0, pl.ds(0, 3)], a1.at[4, pl.ds(0, 3)], prev[0])
        act_corner = send(a1.at[0, 0], a1.at[4, 4], prev[2])
        for i in range(1, 3):
            for j in range(1, 3):
                cell_one(i, j)
        widen_two([(i, j) for i in range(3) for j in range(3)])
        cell_two(0, 0)
        two_row = send(a2.at[0, 0], a2.at[0, 2], prev[1])
        two_plane = send(a2.at[0, 0], a2.at[2, 0], prev[0])
        two_corner = send(a2.at[0, 0], a2.at[2, 2], prev[2])
        got_fg = [send(fgs.at[y], fgs.at[y], device) for device in y_peers]
        widen_three([(0, 0)])

        w3[...] = mm_t(identity(64), w3t[...]).astype(BF16)
        w2rows = w2t[...].reshape(9, 3, 16, 32)
        w3rows = w3t[...].reshape(9, 3, 32, 64)
        for f in range(3):
            w2k[:, f * 32:(f + 1) * 32] = w2rows[:, f].reshape(144, 32)
            w3k[:, f * 64:(f + 1) * 64] = w3rows[:, f].reshape(288, 64)
        row, lane = grid(512, 128)
        regroup = marks(row == (lane >> 5) * 128 + y * 32 + (lane & 31))

        def widen_volume(at, keep):
            part = mm(hr[:, at:at + 32].reshape(128, 256), s1[...]) * keep
            rows = jnp.concatenate(
                [
                    jnp.concatenate(
                        [part[b * 32:(b + 1) * 32, f * 128:(f + 1) * 128] for f in range(3)], axis=0
                    )
                    for b in range(4)
                ],
                axis=1,
            )
            return mm(pm[...], rows.astype(BF16)).astype(BF16).reshape(8, 16, 512)

        arrive(vol_plane)
        e1[8, 0:8] = widen_volume(0, more_x)
        cell_one(3, 0)
        act_row_end = send(a1.at[3, 0], a1.at[3, 4], prev[1])
        arrive(vol_row)
        block = widen_volume(32, more_y)
        for x in range(8):
            e1[x, 8] = block[x]
        cell_one(0, 3)
        act_plane_end = send(a1.at[0, 3], a1.at[4, 3], prev[0])
        for n in range(1, 3):
            cell_one(n, 3)
            cell_one(3, n)
        widen_two([(3, 0), (3, 1), (3, 2)])
        arrive(act_plane)
        widen_two([(4, 0), (4, 1), (4, 2)], more_x)
        cell_two(1, 0)
        two_row_end = send(a2.at[1, 0], a2.at[1, 2], prev[1])
        widen_two([(0, 3), (1, 3), (2, 3)])
        arrive(act_row)
        widen_two([(0, 4), (1, 4), (2, 4)], more_y)
        cell_two(0, 1)
        two_plane_end = send(a2.at[0, 1], a2.at[2, 1], prev[0])
        widen_three([(0, 1), (1, 0)])
        arrive(*got_fg)
        cotangent = mm(jnp.concatenate([fgs[k] for k in range(4)], axis=1), regroup)
        arrive(vol_corner)
        part = mm(hr[:, 64:80].reshape(64, 256), s1[...]) * more_xy
        rows = jnp.concatenate(
            [
                jnp.concatenate(
                    [part[b * 16:(b + 1) * 16, f * 128:(f + 1) * 128] for f in range(3)], axis=0
                )
                for b in range(4)
            ],
            axis=1,
        )
        row, lane = grid(16, 48)
        picked = marks((row == (lane >> 4) * 4 + (lane & 15)) & ((lane & 15) < 4))
        e1[8, 8] = mm(picked, rows.astype(BF16)).astype(BF16)
        cell_one(3, 3)
        widen_two([(3, 3)])
        arrive(act_corner)
        widen_two([(4, 4)], more_xy)
        arrive(act_plane_end)
        widen_two([(4, 3)], more_x)
        arrive(act_row_end)
        widen_two([(3, 4)], more_y)
        cell_two(1, 1)
        got_slope = [
            send(sl2.at[2, pl.ds(1, 2)], sl2.at[0, pl.ds(1, 2)], following[0]),
            send(sl2.at[pl.ds(1, 2), 2], sl2.at[pl.ds(1, 2), 0], following[1]),
            send(sl2.at[2, 2], sl2.at[0, 0], following[2]),
        ]
        widen_three([(1, 1)])
        arrive(two_row, two_row_end)
        widen_three([(0, 2), (1, 2)], more_y)
        arrive(two_plane, two_plane_end)
        widen_three([(2, 0), (2, 1)], more_x)
        arrive(two_corner)
        widen_three([(2, 2)], more_xy)

        columns_three = e3[...].reshape(864, 128)
        act, slope = activate(mm(w3[...], columns_three))
        grad_three = (cotangent * slope.astype(F32)).astype(BF16)
        g3[3] = grad_three
        got_grad = [send(g3.at[3], g3.at[to], following[i]) for i, to in ((2, 0), (1, 2), (0, 1))]

        part = mm_t(columns_three, grad_three)
        part = jnp.concatenate([part[:432], part[432:]], axis=1)
        wb3[...] = jnp.zeros_like(wb3)
        for n in range(27):
            group, at = divmod(n * 16, rows3)
            wb3[group, at:at + 16] = part[n * 16:(n + 1) * 16]
        got_r3 = [send(wb3.at[m], r3.at[d], near[d]) for d, m in enumerate(near_ids)]
        fts[y] = act
        got_feat = [send(fts.at[y], fts.at[y], device) for device in y_peers]

        arrive(*got_grad)
        row, lane = grid(256, 128)
        inside = jnp.where(
            row < 64, less_x * less_y, jnp.where(row < 128, less_x, jnp.where(row < 192, less_y, 1.0))
        )
        rows = (g3[...].reshape(256, 128).astype(F32) * inside).astype(BF16)
        for f in range(3):
            part = mm_t(rows, s3[:, f * 128:(f + 1) * 128]).astype(BF16)
            gg3[:, f * 64:(f + 1) * 64, :] = part.reshape(4, 64, 256)

        def spread(taps, weights, widened, width, channels):
            down = {}
            for i in taps:
                for j in taps:
                    pairs = [(a, e) for a in taps[i] for e in taps[j]]
                    picked = jnp.concatenate(
                        [weights[(a * 3 + e) * channels:(a * 3 + e + 1) * channels, :] for a, e in pairs], axis=0
                    )
                    part = mm(picked, widened[(i + 1) * width + j + 1])
                    for n, (a, e) in enumerate(pairs):
                        key = (2 * i + a, 2 * j + e)
                        term = part[n * channels:(n + 1) * channels]
                        down[key] = term if key not in down else down[key] + term
            return down

        down = spread(TAPS_THREE, w3k, gg3, 2, 32)
        arrive(*got_slope)
        for i in range(-1, 2):
            for j in range(-1, 2):
                rounded = down[i, j].astype(BF16).astype(F32)
                g2e[(i + 1) * 3 + j + 1] = (rounded * sl2[i + 1, j + 1].astype(F32)).astype(BF16)

        part = None
        for i in range(2):
            for j in range(2):
                term = mm_t(columns_two(i, j), g2e[(i + 1) * 3 + j + 1])
                part = term if part is None else part + term
        wb2[...] = jnp.zeros_like(wb2)
        for n in range(54):
            lanes, at = divmod(n * 8, 112)
            group, at = divmod(at, rows2)
            wb2[group, at:at + 8, lanes * 32:(lanes + 1) * 32] = part[n * 8:(n + 1) * 8]
        got_r2 = [send(wb2.at[m], r2.at[d], near[d]) for d, m in enumerate(near_ids)]

        for p in range(2):
            rows = g2e[...].reshape(288, 256)[:, p * 128:(p + 1) * 128]
            for f in range(3):
                part = mm_t(rows, s2[:, f * 128:(f + 1) * 128]).astype(BF16)
                gg2[:, f * 32:(f + 1) * 32, p * 256:(p + 1) * 256] = part.reshape(9, 32, 256)
        down = spread(TAPS_TWO, w2k, gg2, 3, 16)

        part = None
        for i in range(4):
            for j in range(4):
                d1b[(i * 4 + j) * 16:(i * 4 + j + 1) * 16, :] = down[i, j].astype(BF16)
                grad_one = (down[i, j] * sl1[i * 4 + j].astype(F32)).astype(BF16)
                term = mm_t(columns_one(i, j), grad_one)
                part = term if part is None else part + term
        part = jnp.concatenate([part[t * 16:t * 16 + 12] for t in range(9)] + [jnp.zeros((20, 16), F32)], axis=0)
        y1[near_me] = part.T
        got_y1 = [send(y1.at[near_me], y1.at[near_me], device) for device in near]

        def total(first, refs):
            value = first
            for ref in refs:
                value = value + ref
            return value

        arrive(*got_r3)
        z3[far_me] = total(wb3[near_me], [r3[d] for d in range(n_near - 1)])
        got_z3 = [send(z3.at[far_me], z3.at[far_me], device) for device in far]
        row, lane = grid(256, 256)
        swap = marks(((row >> 4) == (lane & 15)) & ((row & 15) == (lane >> 4)))
        block = mm(swap, d1b[...]).astype(BF16)
        for b in range(4):
            gact[b] = block[:, b * 128:(b + 1) * 128]
        store(gact, gact_out)
        arrive(*got_feat)
        feat[...] = mm(jnp.concatenate([fts[k] for k in range(4)], axis=1), regroup).astype(BF16)
        store(feat, feat_out)
        arrive(*got_r2)
        z2[far_me] = total(wb2[near_me], [r2[d] for d in range(n_near - 1)])
        got_z2 = [send(z2.at[far_me], z2.at[far_me], device) for device in far]
        arrive(*got_y1)
        z1[far_me] = total(y1[0], [y1[m] for m in range(1, n_near)])
        got_z1 = [send(z1.at[far_me], z1.at[far_me], device) for device in far]

        arrive(*got_z3)
        f3[near_me] = total(z3[0], [z3[m] for m in range(1, n_far)]) * scales[2]
        got_f3 = [send(f3.at[near_me], f3.at[near_me], device) for device in near]
        arrive(*got_z2)
        f2[near_me] = total(z2[0], [z2[m] for m in range(1, n_far)]) * scales[1]
        got_f2 = [send(f2.at[near_me], f2.at[near_me], device) for device in near]
        arrive(*got_z1)
        part = total(z1[0], [z1[m] for m in range(1, n_far)]) * scales[0]
        o1[...] = part.T[:108].reshape(27, 4, 16)
        store(o1, o1_out)
        arrive(*got_f3)
        part = f3[...].reshape(512, 128)[:432]
        for half in range(2):
            o3[half * 432:(half + 1) * 432, :] = part[:, half * 64:(half + 1) * 64]
        store(o3, o3_out)
        arrive(*got_f2)
        part = f2[...].reshape(128, 128)
        for n in range(27):
            lanes, at = divmod(n * 16, 112)
            o2[n * 16:(n + 1) * 16, :] = part[at:at + 16, lanes * 32:(lanes + 1) * 32]
        store(o2, o2_out)
        for copy in started:
            copy.wait_send()
        for copy in stores:
            copy.wait()

    vm = pltpu.VMEM
    scratch = [
        vm((4, 256, 256), BF16), vm((27, 4, 16), BF16), vm((432, 32), BF16), vm((864, 64), BF16), vm((64, 128), BF16),
        pltpu.SemaphoreType.DMA((5,)),
        vm((64, 128), BF16), vm((4, 256, 128), BF16), vm((27, 4, 16), F32), vm((432, 32), F32), vm((864, 64), F32),
        pltpu.SemaphoreType.DMA((5,)),
        vm((256, 384), BF16), vm((256, 384), BF16), vm((256, 384), BF16), vm((128, 96), BF16),
        vm((16, 144), BF16), vm((32, 432), BF16), vm((64, 864), BF16), vm((144, 96), BF16), vm((288, 192), BF16),
        vm((4, 80, 256), BF16), vm((4, 80, 256), BF16), vm((8, 96, 512), BF16),
        vm((9, 9, 16, 512), BF16), vm((5, 5, 16, 512), BF16), vm((16, 16, 512), BF16), vm((5, 5, 48, 256), BF16),
        vm((3, 3, 32, 256), BF16), vm((3, 3, 32, 256), BF16), vm((3, 3, 96, 128), BF16),
        vm((4, 64, 128), BF16), vm((4, 64, 128), BF16), vm((4, 64, 128), BF16), vm((4, 192, 256), BF16),
        vm((9, 32, 256), BF16), vm((9, 96, 512), BF16), vm((256, 512), BF16),
        vm((n_near, rows3, 128), F32), vm((n_near - 1, rows3, 128), F32), vm((n_far, rows3, 128), F32),
        vm((n_near, rows3, 128), F32),
        vm((n_near, rows2, 128), F32), vm((n_near - 1, rows2, 128), F32), vm((n_far, rows2, 128), F32),
        vm((n_near, rows2, 128), F32),
        vm((n_near, 16, 128), F32), vm((n_far, 16, 128), F32),
        pltpu.SemaphoreType.DMA((COPIES,)), pltpu.SemaphoreType.DMA((COPIES,)),
    ]
    return pl.pallas_call(
        kernel,
        out_shape=(
            jax.ShapeDtypeStruct((64, 128), BF16),
            jax.ShapeDtypeStruct((4, 256, 128), BF16),
            jax.ShapeDtypeStruct((27, 4, 16), F32),
            jax.ShapeDtypeStruct((432, 32), F32),
            jax.ShapeDtypeStruct((864, 64), F32),
        ),
        in_specs=[pl.BlockSpec(memory_space=pltpu.HBM)] * 5,
        out_specs=[pl.BlockSpec(memory_space=pltpu.HBM)] * 5,
        scratch_shapes=scratch,
        compiler_params=pltpu.CompilerParams(
            collective_id=0, has_side_effects=True, vmem_limit_bytes=60 * 1024 * 1024
        ),
        cost_estimate=pl.CostEstimate(flops=3_000_000_000, bytes_accessed=4_000_000, transcendentals=0),
        name="layers",
    )


def hand_over(*refs):
    given, results, held, (sems,) = refs[:5], refs[5:10], refs[10:15], refs[15:]
    come = [pltpu.make_async_copy(given[n], held[n], sems.at[n]) for n in range(5)]
    go = [pltpu.make_async_copy(held[n], results[n], sems.at[5 + n]) for n in range(5)]
    for copy in come:
        copy.start()
    for n in (0, 2, 3, 4, 1):
        come[n].wait()
        go[n].start()
    for copy in go:
        copy.wait()


def solution(mesh):
    ny, ns = mesh.shape["sample"], mesh.shape["space"]
    nx = 4 if ns % 8 == 0 else 2

    def local(volumes, weight_one, weight_two, weight_three, feature_grad):
        cells = volumes.shape[0] * volumes.shape[2] * ns * volumes.shape[3] * ny * volumes.shape[4]
        scales = [GRAD_GAIN / math.sqrt(cells // 8**n) for n in (1, 2, 3)]
        flat = [
            jnp.transpose(w, (2, 3, 4, 1, 0)).reshape(shape)
            for w, shape in ((weight_one, (27, 4, 16)), (weight_two, (432, 32)), (weight_three, (864, 64)))
        ]
        features, grad_act, one, two, three = make_kernel(ny, ns, nx, scales)(
            volumes.reshape(4, 256, 256), *flat, feature_grad.reshape(64, 128)
        )

        features, grad_act, one, two, three = pl.pallas_call(
            hand_over,
            out_shape=(
                jax.ShapeDtypeStruct((64, 128), BF16),
                jax.ShapeDtypeStruct((4, 256, 128), BF16),
                jax.ShapeDtypeStruct((27, 4, 16), F32),
                jax.ShapeDtypeStruct((432, 32), F32),
                jax.ShapeDtypeStruct((864, 64), F32),
            ),
            in_specs=[pl.BlockSpec(memory_space=pltpu.HBM)] * 5,
            out_specs=[pl.BlockSpec(memory_space=pltpu.HBM)] * 5,
            scratch_shapes=[
                pltpu.VMEM((64, 128), BF16), pltpu.VMEM((4, 256, 128), BF16), pltpu.VMEM((27, 4, 16), F32),
                pltpu.VMEM((432, 32), F32), pltpu.VMEM((864, 64), F32), pltpu.SemaphoreType.DMA((10,)),
            ],
            compiler_params=pltpu.CompilerParams(vmem_limit_bytes=63 * 1024 * 1024),
            name="hand_over",
        )(features, grad_act, one, two, three)

        def filters(array, channels):
            return jnp.transpose(array.reshape(3, 3, 3, channels, -1), (4, 3, 0, 1, 2))

        return (
            features.reshape(feature_grad.shape),
            grad_act.reshape(4, 16, 4, 4, 128),
            filters(one, 4),
            filters(two, 16),
            filters(three, 32),
        )

    in_specs = (
        P(None, None, "space", "sample", None),
        P(),
        P(),
        P(),
        P("sample", None, "space", None),
    )
    out_specs = (
        P("sample", None, "space", None),
        P(None, None, "space", "sample", None),
        P(),
        P(),
        P(),
    )
    return jax.shard_map(local, mesh=mesh, in_specs=in_specs, out_specs=out_specs, check_vma=False)
```

```python
import math

import jax
import jax.numpy as jnp
from jax import lax
from jax.experimental import pallas as pl
from jax.experimental.pallas import tpu as pltpu
from jax.sharding import PartitionSpec as P

GRAD_GAIN = 4.0
MESH = pl.DeviceIdType.MESH
F32 = jnp.float32
BF16 = jnp.bfloat16
TAPS_THREE = {-1: (1, 2), 0: (0, 1)}
TAPS_TWO = {-1: (2,), 0: (0, 1, 2), 1: (0, 1)}
COPIES = 29


def mm(a, b):
    return jnp.dot(a, b, preferred_element_type=F32)


def mm_t(a, b):
    return lax.dot_general(a, b, (((1,), (1,)), ((), ())), preferred_element_type=F32)


def activate(p):
    square = p * p + 1.0
    inverse = lax.rsqrt(square)
    active = (0.65 * p + 0.35 * (square * inverse - 1.0)).astype(BF16)
    slope = (0.65 + 0.35 * (p * inverse)).astype(BF16)
    return active, slope


def identity(n):
    return (
        lax.broadcasted_iota(jnp.int32, (n, n), 0) == lax.broadcasted_iota(jnp.int32, (n, n), 1)
    ).astype(F32).astype(BF16)


def grid(rows, lanes):
    return (
        lax.broadcasted_iota(jnp.int32, (rows, lanes), 0),
        lax.broadcasted_iota(jnp.int32, (rows, lanes), 1),
    )


def marks(condition):
    return condition.astype(F32).astype(BF16)


def make_kernel(ny, ns, nx, scales):
    n_near, n_far = ny * nx * 2, ns // (2 * nx)
    rows3, rows2 = 512 // n_near, 128 // n_near

    def kernel(vol_in, w1t_in, w2t_in, w3t_in, fg_in, feat_out, gact_out, o1_out, o2_out, o3_out,
               vol, w1t, w2t, w3t, fg, ls, feat, gact, o1, o2, o3, os,
               s1, s2, s3, pm, w1, w2, w3, w2k, w3k, hs, hr, vsm, e1, a1, sl1, e2, a2, sl2, e3, fgs, fts,
               g3, gg3, g2e, gg2, d1b, wb3, r3, z3, f3, wb2, r2, z2, f2, y1, z1, ss, rs):
        y = lax.axis_index("sample")
        s = lax.axis_index("space")
        z_me = lax.div(s, 2 * nx)
        x_me = lax.div(lax.rem(s, 2 * nx), 2)
        core = lax.rem(s, 2)
        near_me = (y * nx + x_me) * 2 + core
        far_me = z_me
        near_ids = [lax.rem(near_me + d, n_near) for d in range(1, n_near)]
        far_ids = [lax.rem(far_me + d, n_far) for d in range(1, n_far)]
        near = [
            {"sample": lax.div(m, 2 * nx), "space": z_me * 2 * nx + lax.rem(m, 2 * nx)} for m in near_ids
        ]
        far = [{"sample": y, "space": m * 2 * nx + x_me * 2 + core} for m in far_ids]
        y_peers = [{"sample": lax.rem(y + d, ny), "space": s} for d in range(1, ny)]
        y_prev, y_next = lax.rem(y + ny - 1, ny), lax.rem(y + 1, ny)
        s_prev, s_next = lax.rem(s + ns - 1, ns), lax.rem(s + 1, ns)
        prev = [
            {"sample": y, "space": s_prev},
            {"sample": y_prev, "space": s},
            {"sample": y_prev, "space": s_prev},
        ]
        following = [
            {"sample": y, "space": s_next},
            {"sample": y_next, "space": s},
            {"sample": y_next, "space": s_next},
        ]
        started = []
        stores = []
        used = []

        def push(src, dst, device, n):
            copy = pltpu.make_async_remote_copy(
                src_ref=src, dst_ref=dst, send_sem=ss.at[n], recv_sem=rs.at[n],
                device_id=device, device_id_type=MESH,
            )
            copy.start()
            return copy

        def send(src, dst, device):
            used.append(None)
            started.append(push(src, dst, device, len(used) - 1))
            return started[-1]

        def send_all(copies, landed):
            used.append(None)
            n = len(used) - 1
            for src, dst, device in copies:
                push(src, dst, device, n)
            return landed, n

        def arrive_all(group):
            landed, n = group
            pltpu.make_async_copy(landed, landed, rs.at[n]).wait()
            grouped.append(group)

        grouped = []

        def arrive(*copies):
            for copy in copies:
                copy.wait_recv()

        def store(src, dst):
            copy = pltpu.make_async_copy(src, dst, os.at[len(stores)])
            copy.start()
            stores.append(copy)

        barrier = pltpu.get_barrier_semaphore()
        greeted = [prev[0], following[0], prev[2], following[2]] + near + far
        for device in greeted:
            pl.semaphore_signal(barrier, inc=1, device_id=device, device_id_type=MESH)

        loads = {}
        for n, (name, src, dst) in enumerate((
            ("vol", vol_in, vol), ("fg", fg_in, fg), ("w1t", w1t_in, w1t), ("w2t", w2t_in, w2t), ("w3t", w3t_in, w3t),
        )):
            loads[name] = pltpu.make_async_copy(src, dst, ls.at[n])
            loads[name].start()

        def loaded(*names):
            for name in names:
                loads.pop(name).wait()

        more_x = jnp.where(s == ns - 1, 0.0, 1.0).astype(F32)
        more_y = jnp.where(y == ny - 1, 0.0, 1.0).astype(F32)
        less_x = jnp.where(s == 0, 0.0, 1.0).astype(F32)
        less_y = jnp.where(y == 0, 0.0, 1.0).astype(F32)
        more_xy = more_x * more_y

        row, lane = grid(80, 256)
        edge = marks(
            ((row < 32) & (lane == (row >> 3) * 64 + (row & 7)))
            | ((row >= 32) & (row < 64) & (lane == (row - 32) * 8))
            | ((row >= 64) & (row < 68) & (lane == (row - 64) * 64))
        )
        for ref, last in ((s1, 127), (s2, 63), (s3, 31)):
            row, lane = grid(256, 128)
            for f in range(3):
                hit = row == 2 * lane + f
                if f == 2:
                    hit = hit & ((lane & last) != last)
                ref[:, f * 128:(f + 1) * 128] = marks(hit)
        row, lane = grid(128, 96)
        pm[...] = marks(((row & 15) == (lane >> 3)) & ((row >> 4) == (lane & 7)))

        loaded("vol", "fg")
        for b in range(4):
            hs[b] = mm(edge, vol[b]).astype(BF16)
        fgs[y] = fg[...]
        pl.semaphore_wait(barrier, len(greeted))
        vol_row = send(hs.at[:, pl.ds(32, 32)], hr.at[:, pl.ds(32, 32)], prev[1])
        vol_plane = send(hs.at[:, pl.ds(0, 32)], hr.at[:, pl.ds(0, 32)], prev[0])
        vol_corner = send(hs.at[:, pl.ds(64, 16)], hr.at[:, pl.ds(64, 16)], prev[2])

        for b in range(4):
            part = mm(vol[b], s1[...]).reshape(4, 8, 8, 384)
            for x in range(8):
                rows = part[:, x].reshape(32, 384)
                rows = jnp.concatenate([rows[:, f * 128:(f + 1) * 128] for f in range(3)], axis=0)
                vsm[x, :, b * 128:(b + 1) * 128] = rows.astype(BF16)
        for x in range(8):
            e1[x, 0:8] = mm(pm[...], vsm[x]).astype(BF16).reshape(8, 16, 512)
        loaded("w1t", "w2t", "w3t")
        row, lane = grid(144, 108)
        pads = marks((lane == (row >> 4) * 12 + (row & 15)) & ((row & 15) < 12))
        w1rows = w1t[...].astype(F32).reshape(108, 16).astype(BF16)
        w1[...] = mm_t(identity(16), mm(pads, w1rows).astype(BF16)).astype(BF16)
        w2[...] = mm_t(identity(32), w2t[...]).astype(BF16)

        def columns_one(i, j):
            return jnp.concatenate(
                [e1[2 * i + a, 2 * j:2 * j + 3].reshape(48, 512) for a in range(3)], axis=0
            )

        def cell_one(i, j):
            act, slope = activate(mm(w1[...], columns_one(i, j)))
            a1[i, j] = act
            sl1[i * 4 + j] = slope

        def widen_two(cells, keep=None):
            rows = jnp.concatenate([a1[i, j] for i, j in cells], axis=0)
            rows = jnp.concatenate([rows[:, :256], rows[:, 256:]], axis=0)
            part = mm(rows, s2[...])
            if keep is not None:
                part = part * keep
            part = part.astype(BF16).reshape(2, len(cells), 16, 384)
            for p in range(2):
                for n, (i, j) in enumerate(cells):
                    for f in range(3):
                        e2[i, j, f * 16:(f + 1) * 16, p * 128:(p + 1) * 128] = (
                            part[p, n, :, f * 128:(f + 1) * 128]
                        )

        def columns_two(i, j):
            return jnp.concatenate(
                [e2[2 * i + a, 2 * j:2 * j + 3].reshape(144, 256) for a in range(3)], axis=0
            )

        def cell_two(i, j):
            act, slope = activate(mm(w2[...], columns_two(i, j)))
            a2[i, j] = act
            sl2[i + 1, j + 1] = slope

        def widen_three(cells, keep=None):
            part = mm(jnp.concatenate([a2[i, j] for i, j in cells], axis=0), s3[...])
            if keep is not None:
                part = part * keep
            part = part.astype(BF16).reshape(len(cells), 32, 384)
            for n, (i, j) in enumerate(cells):
                for f in range(3):
                    e3[i, j, f * 32:(f + 1) * 32, :] = part[n, :, f * 128:(f + 1) * 128]

        for i in range(3):
            cell_one(i, 0)
        act_row = send(a1.at[pl.ds(0, 3), 0], a1.at[pl.ds(0, 3), 4], prev[1])
        for j in range(1, 3):
            cell_one(0, j)
        act_plane = send(a1.at[0, pl.ds(0, 3)], a1.at[4, pl.ds(0, 3)], prev[0])
        act_corner = send(a1.at[0, 0], a1.at[4, 4], prev[2])
        for i in range(1, 3):
            for j in range(1, 3):
                cell_one(i, j)
        widen_two([(i, j) for i in range(3) for j in range(3)])
        cell_two(0, 0)
        two_row = send(a2.at[0, 0], a2.at[0, 2], prev[1])
        two_plane = send(a2.at[0, 0], a2.at[2, 0], prev[0])
        two_corner = send(a2.at[0, 0], a2.at[2, 2], prev[2])
        got_fg = send_all([(fgs.at[y], fgs.at[y], device) for device in y_peers], fgs.at[pl.ds(0, ny - 1)])
        widen_three([(0, 0)])

        w3[...] = mm_t(identity(64), w3t[...]).astype(BF16)
        w2rows = w2t[...].reshape(9, 3, 16, 32)
        w3rows = w3t[...].reshape(9, 3, 32, 64)
        for f in range(3):
            w2k[:, f * 32:(f + 1) * 32] = w2rows[:, f].reshape(144, 32)
            w3k[:, f * 64:(f + 1) * 64] = w3rows[:, f].reshape(288, 64)
        row, lane = grid(512, 128)
        regroup = marks(row == (lane >> 5) * 128 + y * 32 + (lane & 31))

        def widen_volume(at, keep):
            part = mm(hr[:, at:at + 32].reshape(128, 256), s1[...]) * keep
            rows = jnp.concatenate(
                [
                    jnp.concatenate(
                        [part[b * 32:(b + 1) * 32, f * 128:(f + 1) * 128] for f in range(3)], axis=0
                    )
                    for b in range(4)
                ],
                axis=1,
            )
            return mm(pm[...], rows.astype(BF16)).astype(BF16).reshape(8, 16, 512)

        arrive(vol_plane)
        e1[8, 0:8] = widen_volume(0, more_x)
        cell_one(3, 0)
        act_row_end = send(a1.at[3, 0], a1.at[3, 4], prev[1])
        arrive(vol_row)
        block = widen_volume(32, more_y)
        for x in range(8):
            e1[x, 8] = block[x]
        cell_one(0, 3)
        act_plane_end = send(a1.at[0, 3], a1.at[4, 3], prev[0])
        for n in range(1, 3):
            cell_one(n, 3)
            cell_one(3, n)
        widen_two([(3, 0), (3, 1), (3, 2)])
        arrive(act_plane)
        widen_two([(4, 0), (4, 1), (4, 2)], more_x)
        cell_two(1, 0)
        two_row_end = send(a2.at[1, 0], a2.at[1, 2], prev[1])
        widen_two([(0, 3), (1, 3), (2, 3)])
        arrive(act_row)
        widen_two([(0, 4), (1, 4), (2, 4)], more_y)
        cell_two(0, 1)
        two_plane_end = send(a2.at[0, 1], a2.at[2, 1], prev[0])
        widen_three([(0, 1), (1, 0)])
        arrive_all(got_fg)
        cotangent = mm(jnp.concatenate([fgs[k] for k in range(4)], axis=1), regroup)
        arrive(vol_corner)
        part = mm(hr[:, 64:80].reshape(64, 256), s1[...]) * more_xy
        rows = jnp.concatenate(
            [
                jnp.concatenate(
                    [part[b * 16:(b + 1) * 16, f * 128:(f + 1) * 128] for f in range(3)], axis=0
                )
                for b in range(4)
            ],
            axis=1,
        )
        row, lane = grid(16, 48)
        picked = marks((row == (lane >> 4) * 4 + (lane & 15)) & ((lane & 15) < 4))
        e1[8, 8] = mm(picked, rows.astype(BF16)).astype(BF16)
        cell_one(3, 3)
        widen_two([(3, 3)])
        arrive(act_corner)
        widen_two([(4, 4)], more_xy)
        arrive(act_plane_end)
        widen_two([(4, 3)], more_x)
        arrive(act_row_end)
        widen_two([(3, 4)], more_y)
        cell_two(1, 1)
        got_slope = [
            send(sl2.at[2, pl.ds(1, 2)], sl2.at[0, pl.ds(1, 2)], following[0]),
            send(sl2.at[pl.ds(1, 2), 2], sl2.at[pl.ds(1, 2), 0], following[1]),
            send(sl2.at[2, 2], sl2.at[0, 0], following[2]),
        ]
        widen_three([(1, 1)])
        arrive(two_row, two_row_end)
        widen_three([(0, 2), (1, 2)], more_y)
        arrive(two_plane, two_plane_end)
        widen_three([(2, 0), (2, 1)], more_x)
        arrive(two_corner)
        widen_three([(2, 2)], more_xy)

        columns_three = e3[...].reshape(864, 128)
        act, slope = activate(mm(w3[...], columns_three))
        grad_three = (cotangent * slope.astype(F32)).astype(BF16)
        g3[3] = grad_three
        got_grad = [send(g3.at[3], g3.at[to], following[i]) for i, to in ((2, 0), (1, 2), (0, 1))]

        part = mm_t(columns_three, grad_three)
        part = jnp.concatenate([part[:432], part[432:]], axis=1)
        wb3[...] = jnp.zeros_like(wb3)
        for n in range(27):
            group, at = divmod(n * 16, rows3)
            wb3[group, at:at + 16] = part[n * 16:(n + 1) * 16]
        got_r3 = send_all([(wb3.at[m], r3.at[d], near[d]) for d, m in enumerate(near_ids)], r3)
        fts[y] = act
        got_feat = send_all([(fts.at[y], fts.at[y], device) for device in y_peers], fts.at[pl.ds(0, ny - 1)])

        arrive(*got_grad)
        row, lane = grid(256, 128)
        inside = jnp.where(
            row < 64, less_x * less_y, jnp.where(row < 128, less_x, jnp.where(row < 192, less_y, 1.0))
        )
        rows = (g3[...].reshape(256, 128).astype(F32) * inside).astype(BF16)
        for f in range(3):
            part = mm_t(rows, s3[:, f * 128:(f + 1) * 128]).astype(BF16)
            gg3[:, f * 64:(f + 1) * 64, :] = part.reshape(4, 64, 256)

        def spread(taps, weights, widened, width, channels):
            down = {}
            for i in taps:
                for j in taps:
                    pairs = [(a, e) for a in taps[i] for e in taps[j]]
                    picked = jnp.concatenate(
                        [weights[(a * 3 + e) * channels:(a * 3 + e + 1) * channels, :] for a, e in pairs], axis=0
                    )
                    part = mm(picked, widened[(i + 1) * width + j + 1])
                    for n, (a, e) in enumerate(pairs):
                        key = (2 * i + a, 2 * j + e)
                        term = part[n * channels:(n + 1) * channels]
                        down[key] = term if key not in down else down[key] + term
            return down

        down = spread(TAPS_THREE, w3k, gg3, 2, 32)
        arrive(*got_slope)
        for i in range(-1, 2):
            for j in range(-1, 2):
                rounded = down[i, j].astype(BF16).astype(F32)
                g2e[(i + 1) * 3 + j + 1] = (rounded * sl2[i + 1, j + 1].astype(F32)).astype(BF16)

        part = None
        for i in range(2):
            for j in range(2):
                term = mm_t(columns_two(i, j), g2e[(i + 1) * 3 + j + 1])
                part = term if part is None else part + term
        wb2[...] = jnp.zeros_like(wb2)
        for n in range(432 // rows2):
            lanes, at = divmod(n * rows2, 112)
            wb2[at // rows2, :, lanes * 32:(lanes + 1) * 32] = part[n * rows2:(n + 1) * rows2]
        got_r2 = send_all([(wb2.at[m], r2.at[d], near[d]) for d, m in enumerate(near_ids)], r2)

        for p in range(2):
            rows = g2e[...].reshape(288, 256)[:, p * 128:(p + 1) * 128]
            for f in range(3):
                part = mm_t(rows, s2[:, f * 128:(f + 1) * 128]).astype(BF16)
                gg2[:, f * 32:(f + 1) * 32, p * 256:(p + 1) * 256] = part.reshape(9, 32, 256)
        down = spread(TAPS_TWO, w2k, gg2, 3, 16)

        part = None
        for i in range(4):
            for j in range(4):
                d1b[(i * 4 + j) * 16:(i * 4 + j + 1) * 16, :] = down[i, j].astype(BF16)
                grad_one = (down[i, j] * sl1[i * 4 + j].astype(F32)).astype(BF16)
                term = mm_t(columns_one(i, j), grad_one)
                part = term if part is None else part + term
        part = jnp.concatenate([part[t * 16:t * 16 + 12] for t in range(9)] + [jnp.zeros((20, 16), F32)], axis=0)
        y1[near_me] = part.T
        got_y1 = send_all([(y1.at[near_me], y1.at[near_me], device) for device in near], y1.at[pl.ds(0, n_near - 1)])

        def total(first, refs):
            value = first
            for ref in refs:
                value = value + ref
            return value

        arrive_all(got_r3)
        z3[far_me] = total(wb3[near_me], [r3[d] for d in range(n_near - 1)])
        got_z3 = send_all([(z3.at[far_me], z3.at[far_me], device) for device in far], z3.at[pl.ds(0, n_far - 1)])
        row, lane = grid(256, 256)
        swap = marks(((row >> 4) == (lane & 15)) & ((row & 15) == (lane >> 4)))
        block = mm(swap, d1b[...]).astype(BF16)
        for b in range(4):
            gact[b] = block[:, b * 128:(b + 1) * 128]
        store(gact, gact_out)
        arrive_all(got_feat)
        feat[...] = mm(jnp.concatenate([fts[k] for k in range(4)], axis=1), regroup).astype(BF16)
        store(feat, feat_out)
        arrive_all(got_r2)
        z2[far_me] = total(wb2[near_me], [r2[d] for d in range(n_near - 1)])
        got_z2 = send_all([(z2.at[far_me], z2.at[far_me], device) for device in far], z2.at[pl.ds(0, n_far - 1)])
        arrive_all(got_y1)
        z1[far_me] = total(y1[0], [y1[m] for m in range(1, n_near)])
        got_z1 = send_all([(z1.at[far_me], z1.at[far_me], device) for device in far], z1.at[pl.ds(0, n_far - 1)])

        arrive_all(got_z3)
        f3[near_me] = total(z3[0], [z3[m] for m in range(1, n_far)]) * scales[2]
        got_f3 = send_all([(f3.at[near_me], f3.at[near_me], device) for device in near], f3.at[pl.ds(0, n_near - 1)])
        arrive_all(got_z2)
        f2[near_me] = total(z2[0], [z2[m] for m in range(1, n_far)]) * scales[1]
        got_f2 = send_all([(f2.at[near_me], f2.at[near_me], device) for device in near], f2.at[pl.ds(0, n_near - 1)])
        arrive_all(got_z1)
        part = total(z1[0], [z1[m] for m in range(1, n_far)]) * scales[0]
        o1[...] = part.T[:108].reshape(27, 4, 16)
        store(o1, o1_out)
        arrive_all(got_f3)
        part = f3[...].reshape(512, 128)[:432]
        for half in range(2):
            o3[half * 432:(half + 1) * 432, :] = part[:, half * 64:(half + 1) * 64]
        store(o3, o3_out)
        arrive_all(got_f2)
        part = f2[...].reshape(128, 128)
        for n in range(27):
            lanes, at = divmod(n * 16, 112)
            o2[n * 16:(n + 1) * 16, :] = part[at:at + 16, lanes * 32:(lanes + 1) * 32]
        store(o2, o2_out)
        for copy in started:
            copy.wait_send()
        for landed, n in grouped:
            pltpu.make_async_copy(landed, landed, ss.at[n]).wait()
        for copy in stores:
            copy.wait()

    vm = pltpu.VMEM
    scratch = [
        vm((4, 256, 256), BF16), vm((27, 4, 16), BF16), vm((432, 32), BF16), vm((864, 64), BF16), vm((64, 128), BF16),
        pltpu.SemaphoreType.DMA((5,)),
        vm((64, 128), BF16), vm((4, 256, 128), BF16), vm((27, 4, 16), F32), vm((432, 32), F32), vm((864, 64), F32),
        pltpu.SemaphoreType.DMA((5,)),
        vm((256, 384), BF16), vm((256, 384), BF16), vm((256, 384), BF16), vm((128, 96), BF16),
        vm((16, 144), BF16), vm((32, 432), BF16), vm((64, 864), BF16), vm((144, 96), BF16), vm((288, 192), BF16),
        vm((4, 80, 256), BF16), vm((4, 80, 256), BF16), vm((8, 96, 512), BF16),
        vm((9, 9, 16, 512), BF16), vm((5, 5, 16, 512), BF16), vm((16, 16, 512), BF16), vm((5, 5, 48, 256), BF16),
        vm((3, 3, 32, 256), BF16), vm((3, 3, 32, 256), BF16), vm((3, 3, 96, 128), BF16),
        vm((4, 64, 128), BF16), vm((4, 64, 128), BF16), vm((4, 64, 128), BF16), vm((4, 192, 256), BF16),
        vm((9, 32, 256), BF16), vm((9, 96, 512), BF16), vm((256, 512), BF16),
        vm((n_near, rows3, 128), F32), vm((n_near - 1, rows3, 128), F32), vm((n_far, rows3, 128), F32),
        vm((n_near, rows3, 128), F32),
        vm((n_near, rows2, 128), F32), vm((n_near - 1, rows2, 128), F32), vm((n_far, rows2, 128), F32),
        vm((n_near, rows2, 128), F32),
        vm((n_near, 16, 128), F32), vm((n_far, 16, 128), F32),
        pltpu.SemaphoreType.DMA((COPIES,)), pltpu.SemaphoreType.DMA((COPIES,)),
    ]
    return pl.pallas_call(
        kernel,
        out_shape=(
            jax.ShapeDtypeStruct((64, 128), BF16),
            jax.ShapeDtypeStruct((4, 256, 128), BF16),
            jax.ShapeDtypeStruct((27, 4, 16), F32),
            jax.ShapeDtypeStruct((432, 32), F32),
            jax.ShapeDtypeStruct((864, 64), F32),
        ),
        in_specs=[pl.BlockSpec(memory_space=pltpu.HBM)] * 5,
        out_specs=[pl.BlockSpec(memory_space=pltpu.HBM)] * 5,
        scratch_shapes=scratch,
        compiler_params=pltpu.CompilerParams(
            collective_id=0, has_side_effects=True, vmem_limit_bytes=60 * 1024 * 1024
        ),
        cost_estimate=pl.CostEstimate(flops=3_000_000_000, bytes_accessed=4_000_000, transcendentals=0),
        name="layers",
    )


def hand_over(*refs):
    given, results, held, (sems,) = refs[:5], refs[5:10], refs[10:15], refs[15:]
    come = [pltpu.make_async_copy(given[n], held[n], sems.at[n]) for n in range(5)]
    go = [pltpu.make_async_copy(held[n], results[n], sems.at[5 + n]) for n in range(5)]
    for copy in come:
        copy.start()
    for n in (0, 2, 3, 4, 1):
        come[n].wait()
        go[n].start()
    for copy in go:
        copy.wait()


def solution(mesh):
    ny, ns = mesh.shape["sample"], mesh.shape["space"]
    nx = 4 if ns % 8 == 0 else 1

    def local(volumes, weight_one, weight_two, weight_three, feature_grad):
        cells = volumes.shape[0] * volumes.shape[2] * ns * volumes.shape[3] * ny * volumes.shape[4]
        scales = [GRAD_GAIN / math.sqrt(cells // 8**n) for n in (1, 2, 3)]
        flat = [
            jnp.transpose(w, (2, 3, 4, 1, 0)).reshape(shape)
            for w, shape in ((weight_one, (27, 4, 16)), (weight_two, (432, 32)), (weight_three, (864, 64)))
        ]
        features, grad_act, one, two, three = make_kernel(ny, ns, nx, scales)(
            volumes.reshape(4, 256, 256), *flat, feature_grad.reshape(64, 128)
        )

        features, grad_act, one, two, three = pl.pallas_call(
            hand_over,
            out_shape=(
                jax.ShapeDtypeStruct((64, 128), BF16),
                jax.ShapeDtypeStruct((4, 256, 128), BF16),
                jax.ShapeDtypeStruct((27, 4, 16), F32),
                jax.ShapeDtypeStruct((432, 32), F32),
                jax.ShapeDtypeStruct((864, 64), F32),
            ),
            in_specs=[pl.BlockSpec(memory_space=pltpu.HBM)] * 5,
            out_specs=[pl.BlockSpec(memory_space=pltpu.HBM)] * 5,
            scratch_shapes=[
                pltpu.VMEM((64, 128), BF16), pltpu.VMEM((4, 256, 128), BF16), pltpu.VMEM((27, 4, 16), F32),
                pltpu.VMEM((432, 32), F32), pltpu.VMEM((864, 64), F32), pltpu.SemaphoreType.DMA((10,)),
            ],
            compiler_params=pltpu.CompilerParams(vmem_limit_bytes=63 * 1024 * 1024),
            name="hand_over",
        )(features, grad_act, one, two, three)

        def filters(array, channels):
            return jnp.transpose(array.reshape(3, 3, 3, channels, -1), (4, 3, 0, 1, 2))

        return (
            features.reshape(feature_grad.shape),
            grad_act.reshape(4, 16, 4, 4, 128),
            filters(one, 4),
            filters(two, 16),
            filters(three, 32),
        )

    in_specs = (
        P(None, None, "space", "sample", None),
        P(),
        P(),
        P(),
        P("sample", None, "space", None),
    )
    out_specs = (
        P("sample", None, "space", None),
        P(None, None, "space", "sample", None),
        P(),
        P(),
        P(),
    )
    return jax.shard_map(local, mesh=mesh, in_specs=in_specs, out_specs=out_specs, check_vma=False)
```

```python
import math

import jax
import jax.numpy as jnp
from jax import lax
from jax.experimental import pallas as pl
from jax.experimental.pallas import tpu as pltpu
from jax.sharding import PartitionSpec as P

GRAD_GAIN = 4.0
MESH = pl.DeviceIdType.MESH
F32 = jnp.float32
BF16 = jnp.bfloat16
TAPS_THREE = {-1: (1, 2), 0: (0, 1)}
TAPS_TWO = {-1: (2,), 0: (0, 1, 2), 1: (0, 1)}
COPIES = 29


def mm(a, b):
    return jnp.dot(a, b, preferred_element_type=F32)


def mm_t(a, b):
    return lax.dot_general(a, b, (((1,), (1,)), ((), ())), preferred_element_type=F32)


def activate(p):
    square = p * p + 1.0
    inverse = lax.rsqrt(square)
    active = (0.65 * p + 0.35 * (square * inverse - 1.0)).astype(BF16)
    slope = (0.65 + 0.35 * (p * inverse)).astype(BF16)
    return active, slope


def identity(n):
    return (
        lax.broadcasted_iota(jnp.int32, (n, n), 0) == lax.broadcasted_iota(jnp.int32, (n, n), 1)
    ).astype(F32).astype(BF16)


def grid(rows, lanes):
    return (
        lax.broadcasted_iota(jnp.int32, (rows, lanes), 0),
        lax.broadcasted_iota(jnp.int32, (rows, lanes), 1),
    )


def marks(condition):
    return condition.astype(F32).astype(BF16)


def make_kernel(ny, ns, nx, scales):
    n_near, n_far = ny * nx * 2, ns // (2 * nx)
    rows3, rows2 = 512 // n_near, 128 // n_near

    def kernel(vol_in, w1t_in, w2t_in, w3t_in, fg_in, feat_out, gact_out, o1_out, o2_out, o3_out,
               vol, w1t, w2t, w3t, fg, ls, feat, gact, o1, o2, o3, os,
               s1, s2, s3, pm, w1, w2, w3, w2k, w3k, hs, hr, vsm, e1, a1, sl1, e2, a2, sl2, e3, fgs, fts,
               g3, gg3, g2e, gg2, d1b, wb3, r3, z3, f3, wb2, r2, z2, f2, y1, z1, ss, rs):
        y = lax.axis_index("sample")
        s = lax.axis_index("space")
        z_me = lax.div(s, 2 * nx)
        x_me = lax.div(lax.rem(s, 2 * nx), 2)
        core = lax.rem(s, 2)
        near_me = (y * nx + x_me) * 2 + core
        far_me = z_me
        near_ids = [lax.rem(near_me + d, n_near) for d in range(1, n_near)]
        far_ids = [lax.rem(far_me + d, n_far) for d in range(1, n_far)]
        near = [
            {"sample": lax.div(m, 2 * nx), "space": z_me * 2 * nx + lax.rem(m, 2 * nx)} for m in near_ids
        ]
        far = [{"sample": y, "space": m * 2 * nx + x_me * 2 + core} for m in far_ids]
        y_peers = [{"sample": lax.rem(y + d, ny), "space": s} for d in range(1, ny)]
        y_prev, y_next = lax.rem(y + ny - 1, ny), lax.rem(y + 1, ny)
        s_prev, s_next = lax.rem(s + ns - 1, ns), lax.rem(s + 1, ns)
        prev = [
            {"sample": y, "space": s_prev},
            {"sample": y_prev, "space": s},
            {"sample": y_prev, "space": s_prev},
        ]
        following = [
            {"sample": y, "space": s_next},
            {"sample": y_next, "space": s},
            {"sample": y_next, "space": s_next},
        ]
        started = []
        stores = []
        used = []

        def push(src, dst, device, n):
            copy = pltpu.make_async_remote_copy(
                src_ref=src, dst_ref=dst, send_sem=ss.at[n], recv_sem=rs.at[n],
                device_id=device, device_id_type=MESH,
            )
            copy.start()
            return copy

        def send(src, dst, device):
            used.append(None)
            started.append(push(src, dst, device, len(used) - 1))
            return started[-1]

        def send_all(copies, landed):
            used.append(None)
            n = len(used) - 1
            for src, dst, device in copies:
                push(src, dst, device, n)
            return landed, n

        def arrive_all(group):
            landed, n = group
            pltpu.make_async_copy(landed, landed, rs.at[n]).wait()
            grouped.append(group)

        grouped = []

        def arrive(*copies):
            for copy in copies:
                copy.wait_recv()

        def store(src, dst):
            copy = pltpu.make_async_copy(src, dst, os.at[len(stores)])
            copy.start()
            stores.append(copy)

        barrier = pltpu.get_barrier_semaphore()
        greeted = [prev[0], following[0], prev[2], following[2]] + near + far
        for device in greeted:
            pl.semaphore_signal(barrier, inc=1, device_id=device, device_id_type=MESH)

        loads = {}
        for n, (name, src, dst) in enumerate((
            ("vol", vol_in, vol), ("fg", fg_in, fg), ("w1t", w1t_in, w1t), ("w2t", w2t_in, w2t), ("w3t", w3t_in, w3t),
        )):
            loads[name] = pltpu.make_async_copy(src, dst, ls.at[n])
            loads[name].start()

        def loaded(*names):
            for name in names:
                loads.pop(name).wait()

        more_x = jnp.where(s == ns - 1, 0.0, 1.0).astype(F32)
        more_y = jnp.where(y == ny - 1, 0.0, 1.0).astype(F32)
        less_x = jnp.where(s == 0, 0.0, 1.0).astype(F32)
        less_y = jnp.where(y == 0, 0.0, 1.0).astype(F32)
        more_xy = more_x * more_y

        row, lane = grid(80, 256)
        edge = marks(
            ((row < 32) & (lane == (row >> 3) * 64 + (row & 7)))
            | ((row >= 32) & (row < 64) & (lane == (row - 32) * 8))
            | ((row >= 64) & (row < 68) & (lane == (row - 64) * 64))
        )
        for ref, last in ((s1, 127), (s2, 63), (s3, 31)):
            row, lane = grid(256, 128)
            for f in range(3):
                hit = row == 2 * lane + f
                if f == 2:
                    hit = hit & ((lane & last) != last)
                ref[:, f * 128:(f + 1) * 128] = marks(hit)
        row, lane = grid(128, 96)
        pm[...] = marks(((row & 15) == (lane >> 3)) & ((row >> 4) == (lane & 7)))

        loaded("vol", "fg")
        for b in range(4):
            hs[b] = mm(edge, vol[b]).astype(BF16)
        fgs[y] = fg[...]
        pl.semaphore_wait(barrier, len(greeted))
        vol_row = send(hs.at[:, pl.ds(32, 32)], hr.at[:, pl.ds(32, 32)], prev[1])
        vol_plane = send(hs.at[:, pl.ds(0, 32)], hr.at[:, pl.ds(0, 32)], prev[0])
        vol_corner = send(hs.at[:, pl.ds(64, 16)], hr.at[:, pl.ds(64, 16)], prev[2])

        for b in range(4):
            part = mm(vol[b], s1[...]).reshape(4, 8, 8, 384)
            for x in range(8):
                rows = part[:, x].reshape(32, 384)
                rows = jnp.concatenate([rows[:, f * 128:(f + 1) * 128] for f in range(3)], axis=0)
                vsm[x, :, b * 128:(b + 1) * 128] = rows.astype(BF16)
        for x in range(8):
            e1[x, 0:8] = mm(pm[...], vsm[x]).astype(BF16).reshape(8, 16, 512)
        loaded("w1t", "w2t", "w3t")
        row, lane = grid(144, 108)
        pads = marks((lane == (row >> 4) * 12 + (row & 15)) & ((row & 15) < 12))
        w1rows = w1t[...].astype(F32).reshape(108, 16).astype(BF16)
        w1[...] = mm_t(identity(16), mm(pads, w1rows).astype(BF16)).astype(BF16)
        w2[...] = mm_t(identity(32), w2t[...]).astype(BF16)

        def columns_one(i, j):
            return jnp.concatenate(
                [e1[2 * i + a, 2 * j:2 * j + 3].reshape(48, 512) for a in range(3)], axis=0
            )

        def cell_one(i, j):
            act, slope = activate(mm(w1[...], columns_one(i, j)))
            a1[i, j] = act
            sl1[i * 4 + j] = slope

        def widen_two(cells, keep=None):
            rows = jnp.concatenate([a1[i, j] for i, j in cells], axis=0)
            rows = jnp.concatenate([rows[:, :256], rows[:, 256:]], axis=0)
            part = mm(rows, s2[...])
            if keep is not None:
                part = part * keep
            part = part.astype(BF16).reshape(2, len(cells), 16, 384)
            for p in range(2):
                for n, (i, j) in enumerate(cells):
                    for f in range(3):
                        e2[i, j, f * 16:(f + 1) * 16, p * 128:(p + 1) * 128] = (
                            part[p, n, :, f * 128:(f + 1) * 128]
                        )

        def columns_two(i, j):
            return jnp.concatenate(
                [e2[2 * i + a, 2 * j:2 * j + 3].reshape(144, 256) for a in range(3)], axis=0
            )

        def cell_two(i, j):
            act, slope = activate(mm(w2[...], columns_two(i, j)))
            a2[i, j] = act
            sl2[i + 1, j + 1] = slope

        def widen_three(cells, keep=None):
            part = mm(jnp.concatenate([a2[i, j] for i, j in cells], axis=0), s3[...])
            if keep is not None:
                part = part * keep
            part = part.astype(BF16).reshape(len(cells), 32, 384)
            for n, (i, j) in enumerate(cells):
                for f in range(3):
                    e3[i, j, f * 32:(f + 1) * 32, :] = part[n, :, f * 128:(f + 1) * 128]

        for i in range(3):
            cell_one(i, 0)
        act_row = send(a1.at[pl.ds(0, 3), 0], a1.at[pl.ds(0, 3), 4], prev[1])
        for j in range(1, 3):
            cell_one(0, j)
        act_plane = send(a1.at[0, pl.ds(0, 3)], a1.at[4, pl.ds(0, 3)], prev[0])
        act_corner = send(a1.at[0, 0], a1.at[4, 4], prev[2])
        for i in range(1, 3):
            for j in range(1, 3):
                cell_one(i, j)
        widen_two([(i, j) for i in range(3) for j in range(3)])
        cell_two(0, 0)
        two_row = send(a2.at[0, 0], a2.at[0, 2], prev[1])
        two_plane = send(a2.at[0, 0], a2.at[2, 0], prev[0])
        two_corner = send(a2.at[0, 0], a2.at[2, 2], prev[2])
        got_fg = send_all([(fgs.at[y], fgs.at[y], device) for device in y_peers], fgs.at[pl.ds(0, ny - 1)])
        widen_three([(0, 0)])

        w3[...] = mm_t(identity(64), w3t[...]).astype(BF16)
        w2rows = w2t[...].reshape(9, 3, 16, 32)
        w3rows = w3t[...].reshape(9, 3, 32, 64)
        for f in range(3):
            w2k[:, f * 32:(f + 1) * 32] = w2rows[:, f].reshape(144, 32)
            w3k[:, f * 64:(f + 1) * 64] = w3rows[:, f].reshape(288, 64)
        row, lane = grid(512, 128)
        regroup = marks(row == (lane >> 5) * 128 + y * 32 + (lane & 31))

        def widen_volume(at, keep):
            part = mm(hr[:, at:at + 32].reshape(128, 256), s1[...]) * keep
            rows = jnp.concatenate(
                [
                    jnp.concatenate(
                        [part[b * 32:(b + 1) * 32, f * 128:(f + 1) * 128] for f in range(3)], axis=0
                    )
                    for b in range(4)
                ],
                axis=1,
            )
            return mm(pm[...], rows.astype(BF16)).astype(BF16).reshape(8, 16, 512)

        arrive(vol_plane)
        e1[8, 0:8] = widen_volume(0, more_x)
        cell_one(3, 0)
        act_row_end = send(a1.at[3, 0], a1.at[3, 4], prev[1])
        arrive(vol_row)
        block = widen_volume(32, more_y)
        for x in range(8):
            e1[x, 8] = block[x]
        cell_one(0, 3)
        act_plane_end = send(a1.at[0, 3], a1.at[4, 3], prev[0])
        for n in range(1, 3):
            cell_one(n, 3)
            cell_one(3, n)
        widen_two([(3, 0), (3, 1), (3, 2)])
        arrive(act_plane)
        widen_two([(4, 0), (4, 1), (4, 2)], more_x)
        cell_two(1, 0)
        two_row_end = send(a2.at[1, 0], a2.at[1, 2], prev[1])
        widen_two([(0, 3), (1, 3), (2, 3)])
        arrive(act_row)
        widen_two([(0, 4), (1, 4), (2, 4)], more_y)
        cell_two(0, 1)
        two_plane_end = send(a2.at[0, 1], a2.at[2, 1], prev[0])
        widen_three([(0, 1), (1, 0)])
        arrive_all(got_fg)
        cotangent = mm(jnp.concatenate([fgs[k] for k in range(4)], axis=1), regroup)
        arrive(vol_corner)
        part = mm(hr[:, 64:80].reshape(64, 256), s1[...]) * more_xy
        rows = jnp.concatenate(
            [
                jnp.concatenate(
                    [part[b * 16:(b + 1) * 16, f * 128:(f + 1) * 128] for f in range(3)], axis=0
                )
                for b in range(4)
            ],
            axis=1,
        )
        row, lane = grid(16, 48)
        picked = marks((row == (lane >> 4) * 4 + (lane & 15)) & ((lane & 15) < 4))
        e1[8, 8] = mm(picked, rows.astype(BF16)).astype(BF16)
        cell_one(3, 3)
        widen_two([(3, 3)])
        arrive(act_corner)
        widen_two([(4, 4)], more_xy)
        arrive(act_plane_end)
        widen_two([(4, 3)], more_x)
        arrive(act_row_end)
        widen_two([(3, 4)], more_y)
        cell_two(1, 1)
        got_slope = [
            send(sl2.at[2, pl.ds(1, 2)], sl2.at[0, pl.ds(1, 2)], following[0]),
            send(sl2.at[pl.ds(1, 2), 2], sl2.at[pl.ds(1, 2), 0], following[1]),
            send(sl2.at[2, 2], sl2.at[0, 0], following[2]),
        ]
        widen_three([(1, 1)])
        arrive(two_row, two_row_end)
        widen_three([(0, 2), (1, 2)], more_y)
        arrive(two_plane, two_plane_end)
        widen_three([(2, 0), (2, 1)], more_x)
        arrive(two_corner)
        widen_three([(2, 2)], more_xy)

        columns_three = e3[...].reshape(864, 128)
        act, slope = activate(mm(w3[...], columns_three))
        grad_three = (cotangent * slope.astype(F32)).astype(BF16)
        g3[3] = grad_three
        got_grad = [send(g3.at[3], g3.at[to], following[i]) for i, to in ((2, 0), (1, 2), (0, 1))]

        part = mm_t(columns_three, grad_three)
        part = jnp.concatenate([part[:432], part[432:]], axis=1)
        wb3[...] = jnp.zeros_like(wb3)
        for n in range(27):
            group, at = divmod(n * 16, rows3)
            wb3[group, at:at + 16] = part[n * 16:(n + 1) * 16]
        got_r3 = send_all([(wb3.at[m], r3.at[d], near[d]) for d, m in enumerate(near_ids)], r3)
        fts[y] = act
        got_feat = send_all([(fts.at[y], fts.at[y], device) for device in y_peers], fts.at[pl.ds(0, ny - 1)])

        arrive(*got_grad)
        row, lane = grid(256, 128)
        inside = jnp.where(
            row < 64, less_x * less_y, jnp.where(row < 128, less_x, jnp.where(row < 192, less_y, 1.0))
        )
        rows = (g3[...].reshape(256, 128).astype(F32) * inside).astype(BF16)
        for f in range(3):
            part = mm_t(rows, s3[:, f * 128:(f + 1) * 128]).astype(BF16)
            gg3[:, f * 64:(f + 1) * 64, :] = part.reshape(4, 64, 256)

        def spread(taps, weights, widened, width, channels):
            down = {}
            for i in taps:
                for j in taps:
                    pairs = [(a, e) for a in taps[i] for e in taps[j]]
                    picked = jnp.concatenate(
                        [weights[(a * 3 + e) * channels:(a * 3 + e + 1) * channels, :] for a, e in pairs], axis=0
                    )
                    part = mm(picked, widened[(i + 1) * width + j + 1])
                    for n, (a, e) in enumerate(pairs):
                        key = (2 * i + a, 2 * j + e)
                        term = part[n * channels:(n + 1) * channels]
                        down[key] = term if key not in down else down[key] + term
            return down

        down = spread(TAPS_THREE, w3k, gg3, 2, 32)
        arrive(*got_slope)
        for i in range(-1, 2):
            for j in range(-1, 2):
                rounded = down[i, j].astype(BF16).astype(F32)
                g2e[(i + 1) * 3 + j + 1] = (rounded * sl2[i + 1, j + 1].astype(F32)).astype(BF16)

        part = None
        for i in range(2):
            for j in range(2):
                term = mm_t(columns_two(i, j), g2e[(i + 1) * 3 + j + 1])
                part = term if part is None else part + term
        wb2[...] = jnp.zeros_like(wb2)
        for n in range(432 // rows2):
            lanes, at = divmod(n * rows2, 112)
            wb2[at // rows2, :, lanes * 32:(lanes + 1) * 32] = part[n * rows2:(n + 1) * rows2]
        got_r2 = send_all([(wb2.at[m], r2.at[d], near[d]) for d, m in enumerate(near_ids)], r2)

        for p in range(2):
            rows = g2e[...].reshape(288, 256)[:, p * 128:(p + 1) * 128]
            for f in range(3):
                part = mm_t(rows, s2[:, f * 128:(f + 1) * 128]).astype(BF16)
                gg2[:, f * 32:(f + 1) * 32, p * 256:(p + 1) * 256] = part.reshape(9, 32, 256)
        down = spread(TAPS_TWO, w2k, gg2, 3, 16)

        part = None
        for i in range(4):
            for j in range(4):
                d1b[(i * 4 + j) * 16:(i * 4 + j + 1) * 16, :] = down[i, j].astype(BF16)
                grad_one = (down[i, j] * sl1[i * 4 + j].astype(F32)).astype(BF16)
                term = mm_t(columns_one(i, j), grad_one)
                part = term if part is None else part + term
        part = jnp.concatenate([part[t * 16:t * 16 + 12] for t in range(9)] + [jnp.zeros((20, 16), F32)], axis=0)
        y1[near_me] = part.T
        got_y1 = send_all([(y1.at[near_me], y1.at[near_me], device) for device in near], y1.at[pl.ds(0, n_near - 1)])

        def total(first, refs):
            value = first
            for ref in refs:
                value = value + ref
            return value

        arrive_all(got_r3)
        z3[far_me] = total(wb3[near_me], [r3[d] for d in range(n_near - 1)])
        got_z3 = send_all([(z3.at[far_me], z3.at[far_me], device) for device in far], z3.at[pl.ds(0, n_far - 1)])
        row, lane = grid(256, 256)
        swap = marks(((row >> 4) == (lane & 15)) & ((row & 15) == (lane >> 4)))
        block = mm(swap, d1b[...]).astype(BF16)
        for b in range(4):
            gact[b] = block[:, b * 128:(b + 1) * 128]
        store(gact, gact_out)
        arrive_all(got_feat)
        feat[...] = mm(jnp.concatenate([fts[k] for k in range(4)], axis=1), regroup).astype(BF16)
        store(feat, feat_out)
        arrive_all(got_r2)
        z2[far_me] = total(wb2[near_me], [r2[d] for d in range(n_near - 1)])
        got_z2 = send_all([(z2.at[far_me], z2.at[far_me], device) for device in far], z2.at[pl.ds(0, n_far - 1)])
        arrive_all(got_y1)
        z1[far_me] = total(y1[0], [y1[m] for m in range(1, n_near)])
        got_z1 = send_all([(z1.at[far_me], z1.at[far_me], device) for device in far], z1.at[pl.ds(0, n_far - 1)])

        arrive_all(got_z3)
        f3[near_me] = (total(z3[0], [z3[m] for m in range(1, n_far)]) * scales[2]).astype(BF16)
        got_f3 = send_all([(f3.at[near_me], f3.at[near_me], device) for device in near], f3.at[pl.ds(0, n_near - 1)])
        arrive_all(got_z2)
        f2[near_me] = total(z2[0], [z2[m] for m in range(1, n_far)]) * scales[1]
        got_f2 = send_all([(f2.at[near_me], f2.at[near_me], device) for device in near], f2.at[pl.ds(0, n_near - 1)])
        arrive_all(got_z1)
        part = total(z1[0], [z1[m] for m in range(1, n_far)]) * scales[0]
        o1[...] = part.T[:108].reshape(27, 4, 16)
        store(o1, o1_out)
        arrive_all(got_f3)
        part = f3[...].astype(F32).reshape(512, 128)[:432]
        for half in range(2):
            o3[half * 432:(half + 1) * 432, :] = part[:, half * 64:(half + 1) * 64]
        store(o3, o3_out)
        arrive_all(got_f2)
        part = f2[...].reshape(128, 128)
        for n in range(27):
            lanes, at = divmod(n * 16, 112)
            o2[n * 16:(n + 1) * 16, :] = part[at:at + 16, lanes * 32:(lanes + 1) * 32]
        store(o2, o2_out)
        for copy in started:
            copy.wait_send()
        for landed, n in grouped:
            pltpu.make_async_copy(landed, landed, ss.at[n]).wait()
        for copy in stores:
            copy.wait()

    vm = pltpu.VMEM
    scratch = [
        vm((4, 256, 256), BF16), vm((27, 4, 16), BF16), vm((432, 32), BF16), vm((864, 64), BF16), vm((64, 128), BF16),
        pltpu.SemaphoreType.DMA((5,)),
        vm((64, 128), BF16), vm((4, 256, 128), BF16), vm((27, 4, 16), F32), vm((432, 32), F32), vm((864, 64), F32),
        pltpu.SemaphoreType.DMA((5,)),
        vm((256, 384), BF16), vm((256, 384), BF16), vm((256, 384), BF16), vm((128, 96), BF16),
        vm((16, 144), BF16), vm((32, 432), BF16), vm((64, 864), BF16), vm((144, 96), BF16), vm((288, 192), BF16),
        vm((4, 80, 256), BF16), vm((4, 80, 256), BF16), vm((8, 96, 512), BF16),
        vm((9, 9, 16, 512), BF16), vm((5, 5, 16, 512), BF16), vm((16, 16, 512), BF16), vm((5, 5, 48, 256), BF16),
        vm((3, 3, 32, 256), BF16), vm((3, 3, 32, 256), BF16), vm((3, 3, 96, 128), BF16),
        vm((4, 64, 128), BF16), vm((4, 64, 128), BF16), vm((4, 64, 128), BF16), vm((4, 192, 256), BF16),
        vm((9, 32, 256), BF16), vm((9, 96, 512), BF16), vm((256, 512), BF16),
        vm((n_near, rows3, 128), F32), vm((n_near - 1, rows3, 128), F32), vm((n_far, rows3, 128), F32),
        vm((n_near, rows3, 128), BF16),
        vm((n_near, rows2, 128), F32), vm((n_near - 1, rows2, 128), F32), vm((n_far, rows2, 128), F32),
        vm((n_near, rows2, 128), F32),
        vm((n_near, 16, 128), F32), vm((n_far, 16, 128), F32),
        pltpu.SemaphoreType.DMA((COPIES,)), pltpu.SemaphoreType.DMA((COPIES,)),
    ]
    return pl.pallas_call(
        kernel,
        out_shape=(
            jax.ShapeDtypeStruct((64, 128), BF16),
            jax.ShapeDtypeStruct((4, 256, 128), BF16),
            jax.ShapeDtypeStruct((27, 4, 16), F32),
            jax.ShapeDtypeStruct((432, 32), F32),
            jax.ShapeDtypeStruct((864, 64), F32),
        ),
        in_specs=[pl.BlockSpec(memory_space=pltpu.HBM)] * 5,
        out_specs=[pl.BlockSpec(memory_space=pltpu.HBM)] * 5,
        scratch_shapes=scratch,
        compiler_params=pltpu.CompilerParams(
            collective_id=0, has_side_effects=True, vmem_limit_bytes=60 * 1024 * 1024
        ),
        cost_estimate=pl.CostEstimate(flops=3_000_000_000, bytes_accessed=4_000_000, transcendentals=0),
        name="layers",
    )


def hand_over(*refs):
    given, results, held, (sems,) = refs[:5], refs[5:10], refs[10:15], refs[15:]
    parts = [(n, None) for n in (4, 3, 2, 0)] + [(1, b) for b in range(4)]

    def part(ref, b):
        return ref if b is None else ref.at[b]

    come = [
        pltpu.make_async_copy(part(given[n], b), part(held[n], b), sems.at[k]) for k, (n, b) in enumerate(parts)
    ]
    go = [
        pltpu.make_async_copy(part(held[n], b), part(results[n], b), sems.at[8 + k])
        for k, (n, b) in enumerate(parts)
    ]
    for copy in come:
        copy.start()
    for first, then in zip(come, go):
        first.wait()
        then.start()
    for copy in go:
        copy.wait()


def solution(mesh):
    ny, ns = mesh.shape["sample"], mesh.shape["space"]
    nx = 4 if ns % 8 == 0 else 1

    def local(volumes, weight_one, weight_two, weight_three, feature_grad):
        cells = volumes.shape[0] * volumes.shape[2] * ns * volumes.shape[3] * ny * volumes.shape[4]
        scales = [GRAD_GAIN / math.sqrt(cells // 8**n) for n in (1, 2, 3)]
        flat = [
            jnp.transpose(w, (2, 3, 4, 1, 0)).reshape(shape)
            for w, shape in ((weight_one, (27, 4, 16)), (weight_two, (432, 32)), (weight_three, (864, 64)))
        ]
        features, grad_act, one, two, three = make_kernel(ny, ns, nx, scales)(
            volumes.reshape(4, 256, 256), *flat, feature_grad.reshape(64, 128)
        )

        features, grad_act, one, two, three = pl.pallas_call(
            hand_over,
            out_shape=(
                jax.ShapeDtypeStruct((64, 128), BF16),
                jax.ShapeDtypeStruct((4, 256, 128), BF16),
                jax.ShapeDtypeStruct((27, 4, 16), F32),
                jax.ShapeDtypeStruct((432, 32), F32),
                jax.ShapeDtypeStruct((864, 64), F32),
            ),
            in_specs=[pl.BlockSpec(memory_space=pltpu.HBM)] * 5,
            out_specs=[pl.BlockSpec(memory_space=pltpu.HBM)] * 5,
            scratch_shapes=[
                pltpu.VMEM((64, 128), BF16), pltpu.VMEM((4, 256, 128), BF16), pltpu.VMEM((27, 4, 16), F32),
                pltpu.VMEM((432, 32), F32), pltpu.VMEM((864, 64), F32), pltpu.SemaphoreType.DMA((16,)),
            ],
            compiler_params=pltpu.CompilerParams(vmem_limit_bytes=63 * 1024 * 1024),
            name="hand_over",
        )(features, grad_act, one, two, three)

        def filters(array, channels):
            return jnp.transpose(array.reshape(3, 3, 3, channels, -1), (4, 3, 0, 1, 2))

        return (
            features.reshape(feature_grad.shape),
            grad_act.reshape(4, 16, 4, 4, 128),
            filters(one, 4),
            filters(two, 16),
            filters(three, 32),
        )

    in_specs = (
        P(None, None, "space", "sample", None),
        P(),
        P(),
        P(),
        P("sample", None, "space", None),
    )
    out_specs = (
        P("sample", None, "space", None),
        P(None, None, "space", "sample", None),
        P(),
        P(),
        P(),
    )
    return jax.shard_map(local, mesh=mesh, in_specs=in_specs, out_specs=out_specs, check_vma=False)
```

```python
import math

import jax
import jax.numpy as jnp
from jax import lax
from jax.experimental import pallas as pl
from jax.experimental.pallas import tpu as pltpu
from jax.sharding import PartitionSpec as P

GRAD_GAIN = 4.0
MESH = pl.DeviceIdType.MESH
F32 = jnp.float32
BF16 = jnp.bfloat16
TAPS_THREE = {-1: (1, 2), 0: (0, 1)}
TAPS_TWO = {-1: (2,), 0: (0, 1, 2), 1: (0, 1)}
COPIES = 29


def mm(a, b):
    return jnp.dot(a, b, preferred_element_type=F32)


def mm_t(a, b):
    return lax.dot_general(a, b, (((1,), (1,)), ((), ())), preferred_element_type=F32)


def activate(p):
    square = p * p + 1.0
    inverse = lax.rsqrt(square)
    active = (0.65 * p + 0.35 * (square * inverse - 1.0)).astype(BF16)
    slope = (0.65 + 0.35 * (p * inverse)).astype(BF16)
    return active, slope


def identity(n):
    return (
        lax.broadcasted_iota(jnp.int32, (n, n), 0) == lax.broadcasted_iota(jnp.int32, (n, n), 1)
    ).astype(F32).astype(BF16)


def grid(rows, lanes):
    return (
        lax.broadcasted_iota(jnp.int32, (rows, lanes), 0),
        lax.broadcasted_iota(jnp.int32, (rows, lanes), 1),
    )


def marks(condition):
    return condition.astype(F32).astype(BF16)


def make_kernel(ny, ns, nx, scales):
    n_near, n_far = ny * nx * 2, ns // (2 * nx)
    rows3, rows2 = 512 // n_near, 128 // n_near

    def kernel(vol_in, w1t_in, w2t_in, w3t_in, fg_in, feat_out, gact_out, o1_out, o2_out, o3_out,
               vol, w1t, w2t, w3t, fg, ls, feat, gact, o1, o2, o3, os,
               s1, s2, s3, pm, w1, w2, w3, w2k, w3k, hs, hr, vsm, e1, a1, sl1, e2, a2, sl2, e3, fgs, fts,
               g3, gg3, g2e, gg2, d1b, wb3, r3, z3, f3, wb2, r2, z2, f2, y1, z1, ss, rs):
        y = lax.axis_index("sample")
        s = lax.axis_index("space")
        z_me = lax.div(s, 2 * nx)
        x_me = lax.div(lax.rem(s, 2 * nx), 2)
        core = lax.rem(s, 2)
        near_me = (y * nx + x_me) * 2 + core
        far_me = z_me
        near_ids = [lax.rem(near_me + d, n_near) for d in range(1, n_near)]
        far_ids = [lax.rem(far_me + d, n_far) for d in range(1, n_far)]
        near = [
            {"sample": lax.div(m, 2 * nx), "space": z_me * 2 * nx + lax.rem(m, 2 * nx)} for m in near_ids
        ]
        far = [{"sample": y, "space": m * 2 * nx + x_me * 2 + core} for m in far_ids]
        y_peers = [{"sample": lax.rem(y + d, ny), "space": s} for d in range(1, ny)]
        y_prev, y_next = lax.rem(y + ny - 1, ny), lax.rem(y + 1, ny)
        s_prev, s_next = lax.rem(s + ns - 1, ns), lax.rem(s + 1, ns)
        prev = [
            {"sample": y, "space": s_prev},
            {"sample": y_prev, "space": s},
            {"sample": y_prev, "space": s_prev},
        ]
        following = [
            {"sample": y, "space": s_next},
            {"sample": y_next, "space": s},
            {"sample": y_next, "space": s_next},
        ]
        started = []
        stores = []
        used = []

        def push(src, dst, device, n):
            copy = pltpu.make_async_remote_copy(
                src_ref=src, dst_ref=dst, send_sem=ss.at[n], recv_sem=rs.at[n],
                device_id=device, device_id_type=MESH,
            )
            copy.start()
            return copy

        def send(src, dst, device):
            used.append(None)
            started.append(push(src, dst, device, len(used) - 1))
            return started[-1]

        def send_all(copies, landed):
            used.append(None)
            n = len(used) - 1
            for src, dst, device in copies:
                push(src, dst, device, n)
            return landed, n

        def arrive_all(group):
            landed, n = group
            pltpu.make_async_copy(landed, landed, rs.at[n]).wait()
            grouped.append(group)

        grouped = []

        def arrive(*copies):
            for copy in copies:
                copy.wait_recv()

        def store(src, dst):
            copy = pltpu.make_async_copy(src, dst, os.at[len(stores)])
            copy.start()
            stores.append(copy)

        barrier = pltpu.get_barrier_semaphore()
        greeted = [prev[0], following[0], prev[2], following[2]] + near + far
        for device in greeted:
            pl.semaphore_signal(barrier, inc=1, device_id=device, device_id_type=MESH)

        loads = {}
        for n, (name, src, dst) in enumerate((
            ("vol", vol_in, vol), ("fg", fg_in, fg), ("w1t", w1t_in, w1t), ("w2t", w2t_in, w2t), ("w3t", w3t_in, w3t),
        )):
            loads[name] = pltpu.make_async_copy(src, dst, ls.at[n])
            loads[name].start()

        def loaded(*names):
            for name in names:
                loads.pop(name).wait()

        more_x = jnp.where(s == ns - 1, 0.0, 1.0).astype(F32)
        more_y = jnp.where(y == ny - 1, 0.0, 1.0).astype(F32)
        less_x = jnp.where(s == 0, 0.0, 1.0).astype(F32)
        less_y = jnp.where(y == 0, 0.0, 1.0).astype(F32)
        more_xy = more_x * more_y

        row, lane = grid(80, 256)
        edge = marks(
            ((row < 32) & (lane == (row >> 3) * 64 + (row & 7)))
            | ((row >= 32) & (row < 64) & (lane == (row - 32) * 8))
            | ((row >= 64) & (row < 68) & (lane == (row - 64) * 64))
        )
        for ref, last in ((s1, 127), (s2, 63), (s3, 31)):
            row, lane = grid(256, 128)
            for f in range(3):
                hit = row == 2 * lane + f
                if f == 2:
                    hit = hit & ((lane & last) != last)
                ref[:, f * 128:(f + 1) * 128] = marks(hit)
        row, lane = grid(128, 96)
        pm[...] = marks(((row & 15) == (lane >> 3)) & ((row >> 4) == (lane & 7)))

        loaded("vol", "fg")
        for b in range(4):
            hs[b] = mm(edge, vol[b]).astype(BF16)
        fgs[y] = fg[...]
        pl.semaphore_wait(barrier, len(greeted))
        vol_row = send(hs.at[:, pl.ds(32, 32)], hr.at[:, pl.ds(32, 32)], prev[1])
        vol_plane = send(hs.at[:, pl.ds(0, 32)], hr.at[:, pl.ds(0, 32)], prev[0])
        vol_corner = send(hs.at[:, pl.ds(64, 16)], hr.at[:, pl.ds(64, 16)], prev[2])

        for b in range(4):
            part = mm(vol[b], s1[...]).reshape(4, 8, 8, 384)
            for x in range(8):
                rows = part[:, x].reshape(32, 384)
                rows = jnp.concatenate([rows[:, f * 128:(f + 1) * 128] for f in range(3)], axis=0)
                vsm[x, :, b * 128:(b + 1) * 128] = rows.astype(BF16)
        for x in range(8):
            e1[x, 0:8] = mm(pm[...], vsm[x]).astype(BF16).reshape(8, 16, 512)
        loaded("w1t", "w2t", "w3t")
        row, lane = grid(144, 108)
        pads = marks((lane == (row >> 4) * 12 + (row & 15)) & ((row & 15) < 12))
        w1rows = w1t[...].astype(F32).reshape(108, 16).astype(BF16)
        w1[...] = mm_t(identity(16), mm(pads, w1rows).astype(BF16)).astype(BF16)
        w2[...] = mm_t(identity(32), w2t[...]).astype(BF16)

        def columns_one(i, j):
            return jnp.concatenate(
                [e1[2 * i + a, 2 * j:2 * j + 3].reshape(48, 512) for a in range(3)], axis=0
            )

        def cell_one(i, j):
            act, slope = activate(mm(w1[...], columns_one(i, j)))
            a1[i, j] = act
            sl1[i * 4 + j] = slope

        def widen_two(cells, keep=None):
            rows = jnp.concatenate([a1[i, j] for i, j in cells], axis=0)
            rows = jnp.concatenate([rows[:, :256], rows[:, 256:]], axis=0)
            part = mm(rows, s2[...])
            if keep is not None:
                part = part * keep
            part = part.astype(BF16).reshape(2, len(cells), 16, 384)
            for p in range(2):
                for n, (i, j) in enumerate(cells):
                    for f in range(3):
                        e2[i, j, f * 16:(f + 1) * 16, p * 128:(p + 1) * 128] = (
                            part[p, n, :, f * 128:(f + 1) * 128]
                        )

        def columns_two(i, j):
            return jnp.concatenate(
                [e2[2 * i + a, 2 * j:2 * j + 3].reshape(144, 256) for a in range(3)], axis=0
            )

        def cell_two(i, j):
            act, slope = activate(mm(w2[...], columns_two(i, j)))
            a2[i, j] = act
            sl2[i + 1, j + 1] = slope

        def widen_three(cells, keep=None):
            part = mm(jnp.concatenate([a2[i, j] for i, j in cells], axis=0), s3[...])
            if keep is not None:
                part = part * keep
            part = part.astype(BF16).reshape(len(cells), 32, 384)
            for n, (i, j) in enumerate(cells):
                for f in range(3):
                    e3[i, j, f * 32:(f + 1) * 32, :] = part[n, :, f * 128:(f + 1) * 128]

        for i in range(3):
            cell_one(i, 0)
        act_row = send(a1.at[pl.ds(0, 3), 0], a1.at[pl.ds(0, 3), 4], prev[1])
        for j in range(1, 3):
            cell_one(0, j)
        act_plane = send(a1.at[0, pl.ds(0, 3)], a1.at[4, pl.ds(0, 3)], prev[0])
        act_corner = send(a1.at[0, 0], a1.at[4, 4], prev[2])
        for i in range(1, 3):
            for j in range(1, 3):
                cell_one(i, j)
        widen_two([(i, j) for i in range(3) for j in range(3)])
        cell_two(0, 0)
        two_row = send(a2.at[0, 0], a2.at[0, 2], prev[1])
        two_plane = send(a2.at[0, 0], a2.at[2, 0], prev[0])
        two_corner = send(a2.at[0, 0], a2.at[2, 2], prev[2])
        got_fg = send_all([(fgs.at[y], fgs.at[y], device) for device in y_peers], fgs.at[pl.ds(0, ny - 1)])
        widen_three([(0, 0)])

        w3[...] = mm_t(identity(64), w3t[...]).astype(BF16)
        w2rows = w2t[...].reshape(9, 3, 16, 32)
        w3rows = w3t[...].reshape(9, 3, 32, 64)
        for f in range(3):
            w2k[:, f * 32:(f + 1) * 32] = w2rows[:, f].reshape(144, 32)
            w3k[:, f * 64:(f + 1) * 64] = w3rows[:, f].reshape(288, 64)
        row, lane = grid(512, 128)
        regroup = marks(row == (lane >> 5) * 128 + y * 32 + (lane & 31))

        def widen_volume(at, keep):
            part = mm(hr[:, at:at + 32].reshape(128, 256), s1[...]) * keep
            rows = jnp.concatenate(
                [
                    jnp.concatenate(
                        [part[b * 32:(b + 1) * 32, f * 128:(f + 1) * 128] for f in range(3)], axis=0
                    )
                    for b in range(4)
                ],
                axis=1,
            )
            return mm(pm[...], rows.astype(BF16)).astype(BF16).reshape(8, 16, 512)

        arrive(vol_plane)
        e1[8, 0:8] = widen_volume(0, more_x)
        cell_one(3, 0)
        act_row_end = send(a1.at[3, 0], a1.at[3, 4], prev[1])
        arrive(vol_row)
        block = widen_volume(32, more_y)
        for x in range(8):
            e1[x, 8] = block[x]
        cell_one(0, 3)
        act_plane_end = send(a1.at[0, 3], a1.at[4, 3], prev[0])
        for n in range(1, 3):
            cell_one(n, 3)
            cell_one(3, n)
        widen_two([(3, 0), (3, 1), (3, 2)])
        arrive(act_plane)
        widen_two([(4, 0), (4, 1), (4, 2)], more_x)
        cell_two(1, 0)
        two_row_end = send(a2.at[1, 0], a2.at[1, 2], prev[1])
        widen_two([(0, 3), (1, 3), (2, 3)])
        arrive(act_row)
        widen_two([(0, 4), (1, 4), (2, 4)], more_y)
        cell_two(0, 1)
        two_plane_end = send(a2.at[0, 1], a2.at[2, 1], prev[0])
        widen_three([(0, 1), (1, 0)])
        arrive_all(got_fg)
        cotangent = mm(jnp.concatenate([fgs[k] for k in range(4)], axis=1), regroup)
        arrive(vol_corner)
        part = mm(hr[:, 64:80].reshape(64, 256), s1[...]) * more_xy
        rows = jnp.concatenate(
            [
                jnp.concatenate(
                    [part[b * 16:(b + 1) * 16, f * 128:(f + 1) * 128] for f in range(3)], axis=0
                )
                for b in range(4)
            ],
            axis=1,
        )
        row, lane = grid(16, 48)
        picked = marks((row == (lane >> 4) * 4 + (lane & 15)) & ((lane & 15) < 4))
        e1[8, 8] = mm(picked, rows.astype(BF16)).astype(BF16)
        cell_one(3, 3)
        widen_two([(3, 3)])
        arrive(act_corner)
        widen_two([(4, 4)], more_xy)
        arrive(act_plane_end)
        widen_two([(4, 3)], more_x)
        arrive(act_row_end)
        widen_two([(3, 4)], more_y)
        cell_two(1, 1)
        got_slope = [
            send(sl2.at[2, pl.ds(1, 2)], sl2.at[0, pl.ds(1, 2)], following[0]),
            send(sl2.at[pl.ds(1, 2), 2], sl2.at[pl.ds(1, 2), 0], following[1]),
            send(sl2.at[2, 2], sl2.at[0, 0], following[2]),
        ]
        widen_three([(1, 1)])
        arrive(two_row, two_row_end)
        widen_three([(0, 2), (1, 2)], more_y)
        arrive(two_plane, two_plane_end)
        widen_three([(2, 0), (2, 1)], more_x)
        arrive(two_corner)
        widen_three([(2, 2)], more_xy)

        columns_three = e3[...].reshape(864, 128)
        act, slope = activate(mm(w3[...], columns_three))
        grad_three = (cotangent * slope.astype(F32)).astype(BF16)
        g3[3] = grad_three
        got_grad = [send(g3.at[3], g3.at[to], following[i]) for i, to in ((2, 0), (1, 2), (0, 1))]

        part = mm_t(columns_three, grad_three)
        part = jnp.concatenate([part[:432], part[432:]], axis=1).astype(BF16)
        wb3[...] = jnp.zeros_like(wb3)
        for n in range(27):
            group, at = divmod(n * 16, rows3)
            wb3[group, at:at + 16] = part[n * 16:(n + 1) * 16]
        got_r3 = send_all([(wb3.at[m], r3.at[d], near[d]) for d, m in enumerate(near_ids)], r3)
        fts[y] = act
        got_feat = send_all([(fts.at[y], fts.at[y], device) for device in y_peers], fts.at[pl.ds(0, ny - 1)])

        arrive(*got_grad)
        row, lane = grid(256, 128)
        inside = jnp.where(
            row < 64, less_x * less_y, jnp.where(row < 128, less_x, jnp.where(row < 192, less_y, 1.0))
        )
        rows = (g3[...].reshape(256, 128).astype(F32) * inside).astype(BF16)
        for f in range(3):
            part = mm_t(rows, s3[:, f * 128:(f + 1) * 128]).astype(BF16)
            gg3[:, f * 64:(f + 1) * 64, :] = part.reshape(4, 64, 256)

        def spread(taps, weights, widened, width, channels):
            down = {}
            for i in taps:
                for j in taps:
                    pairs = [(a, e) for a in taps[i] for e in taps[j]]
                    picked = jnp.concatenate(
                        [weights[(a * 3 + e) * channels:(a * 3 + e + 1) * channels, :] for a, e in pairs], axis=0
                    )
                    part = mm(picked, widened[(i + 1) * width + j + 1])
                    for n, (a, e) in enumerate(pairs):
                        key = (2 * i + a, 2 * j + e)
                        term = part[n * channels:(n + 1) * channels]
                        down[key] = term if key not in down else down[key] + term
            return down

        down = spread(TAPS_THREE, w3k, gg3, 2, 32)
        arrive(*got_slope)
        for i in range(-1, 2):
            for j in range(-1, 2):
                rounded = down[i, j].astype(BF16).astype(F32)
                g2e[(i + 1) * 3 + j + 1] = (rounded * sl2[i + 1, j + 1].astype(F32)).astype(BF16)

        part = None
        for i in range(2):
            for j in range(2):
                term = mm_t(columns_two(i, j), g2e[(i + 1) * 3 + j + 1])
                part = term if part is None else part + term
        wb2[...] = jnp.zeros_like(wb2)
        for n in range(432 // rows2):
            lanes, at = divmod(n * rows2, 112)
            wb2[at // rows2, :, lanes * 32:(lanes + 1) * 32] = part[n * rows2:(n + 1) * rows2]
        got_r2 = send_all([(wb2.at[m], r2.at[d], near[d]) for d, m in enumerate(near_ids)], r2)

        for p in range(2):
            rows = g2e[...].reshape(288, 256)[:, p * 128:(p + 1) * 128]
            for f in range(3):
                part = mm_t(rows, s2[:, f * 128:(f + 1) * 128]).astype(BF16)
                gg2[:, f * 32:(f + 1) * 32, p * 256:(p + 1) * 256] = part.reshape(9, 32, 256)
        down = spread(TAPS_TWO, w2k, gg2, 3, 16)

        part = None
        for i in range(4):
            for j in range(4):
                d1b[(i * 4 + j) * 16:(i * 4 + j + 1) * 16, :] = down[i, j].astype(BF16)
                grad_one = (down[i, j] * sl1[i * 4 + j].astype(F32)).astype(BF16)
                term = mm_t(columns_one(i, j), grad_one)
                part = term if part is None else part + term
        part = jnp.concatenate([part[t * 16:t * 16 + 12] for t in range(9)] + [jnp.zeros((20, 16), F32)], axis=0)
        y1[near_me] = part.T.astype(BF16)
        got_y1 = send_all([(y1.at[near_me], y1.at[near_me], device) for device in near], y1.at[pl.ds(0, n_near - 1)])

        def total(first, refs):
            value = first.astype(F32)
            for ref in refs:
                value = value + ref.astype(F32)
            return value

        arrive_all(got_r3)
        z3[far_me] = total(wb3[near_me], [r3[d] for d in range(n_near - 1)])
        got_z3 = send_all([(z3.at[far_me], z3.at[far_me], device) for device in far], z3.at[pl.ds(0, n_far - 1)])
        row, lane = grid(256, 256)
        swap = marks(((row >> 4) == (lane & 15)) & ((row & 15) == (lane >> 4)))
        block = mm(swap, d1b[...]).astype(BF16)
        for b in range(4):
            gact[b] = block[:, b * 128:(b + 1) * 128]
        store(gact, gact_out)
        arrive_all(got_feat)
        feat[...] = mm(jnp.concatenate([fts[k] for k in range(4)], axis=1), regroup).astype(BF16)
        store(feat, feat_out)
        arrive_all(got_r2)
        z2[far_me] = total(wb2[near_me], [r2[d] for d in range(n_near - 1)])
        got_z2 = send_all([(z2.at[far_me], z2.at[far_me], device) for device in far], z2.at[pl.ds(0, n_far - 1)])
        arrive_all(got_y1)
        z1[far_me] = total(y1[0], [y1[m] for m in range(1, n_near)])
        got_z1 = send_all([(z1.at[far_me], z1.at[far_me], device) for device in far], z1.at[pl.ds(0, n_far - 1)])

        arrive_all(got_z3)
        f3[near_me] = (total(z3[0], [z3[m] for m in range(1, n_far)]) * scales[2]).astype(BF16)
        got_f3 = send_all([(f3.at[near_me], f3.at[near_me], device) for device in near], f3.at[pl.ds(0, n_near - 1)])
        arrive_all(got_z2)
        f2[near_me] = total(z2[0], [z2[m] for m in range(1, n_far)]) * scales[1]
        got_f2 = send_all([(f2.at[near_me], f2.at[near_me], device) for device in near], f2.at[pl.ds(0, n_near - 1)])
        arrive_all(got_z1)
        part = total(z1[0], [z1[m] for m in range(1, n_far)]) * scales[0]
        o1[...] = part.T[:108].reshape(27, 4, 16)
        store(o1, o1_out)
        arrive_all(got_f3)
        part = f3[...].astype(F32).reshape(512, 128)[:432]
        for half in range(2):
            o3[half * 432:(half + 1) * 432, :] = part[:, half * 64:(half + 1) * 64]
        store(o3, o3_out)
        arrive_all(got_f2)
        part = f2[...].reshape(128, 128)
        for n in range(27):
            lanes, at = divmod(n * 16, 112)
            o2[n * 16:(n + 1) * 16, :] = part[at:at + 16, lanes * 32:(lanes + 1) * 32]
        store(o2, o2_out)
        for copy in started:
            copy.wait_send()
        for landed, n in grouped:
            pltpu.make_async_copy(landed, landed, ss.at[n]).wait()
        for copy in stores:
            copy.wait()

    vm = pltpu.VMEM
    scratch = [
        vm((4, 256, 256), BF16), vm((27, 4, 16), BF16), vm((432, 32), BF16), vm((864, 64), BF16), vm((64, 128), BF16),
        pltpu.SemaphoreType.DMA((5,)),
        vm((64, 128), BF16), vm((4, 256, 128), BF16), vm((27, 4, 16), F32), vm((432, 32), F32), vm((864, 64), F32),
        pltpu.SemaphoreType.DMA((5,)),
        vm((256, 384), BF16), vm((256, 384), BF16), vm((256, 384), BF16), vm((128, 96), BF16),
        vm((16, 144), BF16), vm((32, 432), BF16), vm((64, 864), BF16), vm((144, 96), BF16), vm((288, 192), BF16),
        vm((4, 80, 256), BF16), vm((4, 80, 256), BF16), vm((8, 96, 512), BF16),
        vm((9, 9, 16, 512), BF16), vm((5, 5, 16, 512), BF16), vm((16, 16, 512), BF16), vm((5, 5, 48, 256), BF16),
        vm((3, 3, 32, 256), BF16), vm((3, 3, 32, 256), BF16), vm((3, 3, 96, 128), BF16),
        vm((4, 64, 128), BF16), vm((4, 64, 128), BF16), vm((4, 64, 128), BF16), vm((4, 192, 256), BF16),
        vm((9, 32, 256), BF16), vm((9, 96, 512), BF16), vm((256, 512), BF16),
        vm((n_near, rows3, 128), BF16), vm((n_near - 1, rows3, 128), BF16), vm((n_far, rows3, 128), F32),
        vm((n_near, rows3, 128), BF16),
        vm((n_near, rows2, 128), F32), vm((n_near - 1, rows2, 128), F32), vm((n_far, rows2, 128), F32),
        vm((n_near, rows2, 128), F32),
        vm((n_near, 16, 128), BF16), vm((n_far, 16, 128), F32),
        pltpu.SemaphoreType.DMA((COPIES,)), pltpu.SemaphoreType.DMA((COPIES,)),
    ]
    return pl.pallas_call(
        kernel,
        out_shape=(
            jax.ShapeDtypeStruct((64, 128), BF16),
            jax.ShapeDtypeStruct((4, 256, 128), BF16),
            jax.ShapeDtypeStruct((27, 4, 16), F32),
            jax.ShapeDtypeStruct((432, 32), F32),
            jax.ShapeDtypeStruct((864, 64), F32),
        ),
        in_specs=[pl.BlockSpec(memory_space=pltpu.HBM)] * 5,
        out_specs=[pl.BlockSpec(memory_space=pltpu.HBM)] * 5,
        scratch_shapes=scratch,
        compiler_params=pltpu.CompilerParams(
            collective_id=0, has_side_effects=True, vmem_limit_bytes=60 * 1024 * 1024
        ),
        cost_estimate=pl.CostEstimate(flops=3_000_000_000, bytes_accessed=4_000_000, transcendentals=0),
        name="layers",
    )


def hand_over(*refs):
    given, results, held, (sems,) = refs[:5], refs[5:10], refs[10:15], refs[15:]
    parts = [(n, None) for n in (4, 3, 2, 0)] + [(1, b) for b in range(4)]

    def part(ref, b):
        return ref if b is None else ref.at[b]

    come = [
        pltpu.make_async_copy(part(given[n], b), part(held[n], b), sems.at[k]) for k, (n, b) in enumerate(parts)
    ]
    go = [
        pltpu.make_async_copy(part(held[n], b), part(results[n], b), sems.at[8 + k])
        for k, (n, b) in enumerate(parts)
    ]
    for copy in come:
        copy.start()
    for first, then in zip(come, go):
        first.wait()
        then.start()
    for copy in go:
        copy.wait()


def solution(mesh):
    ny, ns = mesh.shape["sample"], mesh.shape["space"]
    nx = 4 if ns % 8 == 0 else 1

    def local(volumes, weight_one, weight_two, weight_three, feature_grad):
        cells = volumes.shape[0] * volumes.shape[2] * ns * volumes.shape[3] * ny * volumes.shape[4]
        scales = [GRAD_GAIN / math.sqrt(cells // 8**n) for n in (1, 2, 3)]
        flat = [
            jnp.transpose(w, (2, 3, 4, 1, 0)).reshape(shape)
            for w, shape in ((weight_one, (27, 4, 16)), (weight_two, (432, 32)), (weight_three, (864, 64)))
        ]
        features, grad_act, one, two, three = make_kernel(ny, ns, nx, scales)(
            volumes.reshape(4, 256, 256), *flat, feature_grad.reshape(64, 128)
        )

        features, grad_act, one, two, three = pl.pallas_call(
            hand_over,
            out_shape=(
                jax.ShapeDtypeStruct((64, 128), BF16),
                jax.ShapeDtypeStruct((4, 256, 128), BF16),
                jax.ShapeDtypeStruct((27, 4, 16), F32),
                jax.ShapeDtypeStruct((432, 32), F32),
                jax.ShapeDtypeStruct((864, 64), F32),
            ),
            in_specs=[pl.BlockSpec(memory_space=pltpu.HBM)] * 5,
            out_specs=[pl.BlockSpec(memory_space=pltpu.HBM)] * 5,
            scratch_shapes=[
                pltpu.VMEM((64, 128), BF16), pltpu.VMEM((4, 256, 128), BF16), pltpu.VMEM((27, 4, 16), F32),
                pltpu.VMEM((432, 32), F32), pltpu.VMEM((864, 64), F32), pltpu.SemaphoreType.DMA((16,)),
            ],
            compiler_params=pltpu.CompilerParams(vmem_limit_bytes=63 * 1024 * 1024),
            name="hand_over",
        )(features, grad_act, one, two, three)

        def filters(array, channels):
            return jnp.transpose(array.reshape(3, 3, 3, channels, -1), (4, 3, 0, 1, 2))

        return (
            features.reshape(feature_grad.shape),
            grad_act.reshape(4, 16, 4, 4, 128),
            filters(one, 4),
            filters(two, 16),
            filters(three, 32),
        )

    in_specs = (
        P(None, None, "space", "sample", None),
        P(),
        P(),
        P(),
        P("sample", None, "space", None),
    )
    out_specs = (
        P("sample", None, "space", None),
        P(None, None, "space", "sample", None),
        P(),
        P(),
        P(),
    )
    return jax.shard_map(local, mesh=mesh, in_specs=in_specs, out_specs=out_specs, check_vma=False)
```

```python
import math

import jax
import jax.numpy as jnp
from jax import lax
from jax.experimental import pallas as pl
from jax.experimental.pallas import tpu as pltpu
from jax.sharding import PartitionSpec as P

GRAD_GAIN = 4.0
MESH = pl.DeviceIdType.MESH
F32 = jnp.float32
BF16 = jnp.bfloat16
TAPS_THREE = {-1: (1, 2), 0: (0, 1)}
TAPS_TWO = {-1: (2,), 0: (0, 1, 2), 1: (0, 1)}
COPIES = 29


def mm(a, b):
    return jnp.dot(a, b, preferred_element_type=F32)


def mm_t(a, b):
    return lax.dot_general(a, b, (((1,), (1,)), ((), ())), preferred_element_type=F32)


def activate(p):
    square = p * p + 1.0
    inverse = lax.rsqrt(square)
    active = (0.65 * p + 0.35 * (square * inverse - 1.0)).astype(BF16)
    slope = (0.65 + 0.35 * (p * inverse)).astype(BF16)
    return active, slope


def identity(n):
    return (
        lax.broadcasted_iota(jnp.int32, (n, n), 0) == lax.broadcasted_iota(jnp.int32, (n, n), 1)
    ).astype(F32).astype(BF16)


def grid(rows, lanes):
    return (
        lax.broadcasted_iota(jnp.int32, (rows, lanes), 0),
        lax.broadcasted_iota(jnp.int32, (rows, lanes), 1),
    )


def marks(condition):
    return condition.astype(F32).astype(BF16)


def make_kernel(ny, ns, nx, scales):
    n_near, n_far = ny * nx * 2, ns // (2 * nx)
    rows3, rows2 = 512 // n_near, 128 // n_near

    def kernel(vol_in, w1t_in, w2t_in, w3t_in, fg_in, feat_out, gact_out, o1_out, o2_out, o3_out,
               vol, w1t, w2t, w3t, fg, ls, feat, gact, o1, os,
               s1, s2, s3, pm, w1, w2, w3, w2k, w3k, hs, hr, vsm, e1, a1, sl1, e2, a2, sl2, e3, fgs, fts,
               g3, gg3, g2e, gg2, d1b, wb3, r3, z3, f3, wb2, r2, z2, f2, y1, z1, ss, rs):
        y = lax.axis_index("sample")
        s = lax.axis_index("space")
        z_me = lax.div(s, 2 * nx)
        x_me = lax.div(lax.rem(s, 2 * nx), 2)
        core = lax.rem(s, 2)
        near_me = (y * nx + x_me) * 2 + core
        far_me = z_me
        near_ids = [lax.rem(near_me + d, n_near) for d in range(1, n_near)]
        far_ids = [lax.rem(far_me + d, n_far) for d in range(1, n_far)]
        near = [
            {"sample": lax.div(m, 2 * nx), "space": z_me * 2 * nx + lax.rem(m, 2 * nx)} for m in near_ids
        ]
        far = [{"sample": y, "space": m * 2 * nx + x_me * 2 + core} for m in far_ids]
        y_peers = [{"sample": lax.rem(y + d, ny), "space": s} for d in range(1, ny)]
        y_prev, y_next = lax.rem(y + ny - 1, ny), lax.rem(y + 1, ny)
        s_prev, s_next = lax.rem(s + ns - 1, ns), lax.rem(s + 1, ns)
        prev = [
            {"sample": y, "space": s_prev},
            {"sample": y_prev, "space": s},
            {"sample": y_prev, "space": s_prev},
        ]
        following = [
            {"sample": y, "space": s_next},
            {"sample": y_next, "space": s},
            {"sample": y_next, "space": s_next},
        ]
        started = []
        stores = []
        used = []

        def push(src, dst, device, n):
            copy = pltpu.make_async_remote_copy(
                src_ref=src, dst_ref=dst, send_sem=ss.at[n], recv_sem=rs.at[n],
                device_id=device, device_id_type=MESH,
            )
            copy.start()
            return copy

        def send(src, dst, device):
            used.append(None)
            started.append(push(src, dst, device, len(used) - 1))
            return started[-1]

        def send_all(copies, landed):
            used.append(None)
            n = len(used) - 1
            for src, dst, device in copies:
                push(src, dst, device, n)
            return landed, n

        def arrive_all(group):
            landed, n = group
            pltpu.make_async_copy(landed, landed, rs.at[n]).wait()
            grouped.append(group)

        grouped = []

        def arrive(*copies):
            for copy in copies:
                copy.wait_recv()

        def store(src, dst):
            copy = pltpu.make_async_copy(src, dst, os.at[len(stores)])
            copy.start()
            stores.append(copy)

        barrier = pltpu.get_barrier_semaphore()
        greeted = [prev[0], following[0], prev[2], following[2]] + near + far
        for device in greeted:
            pl.semaphore_signal(barrier, inc=1, device_id=device, device_id_type=MESH)

        loads = {}
        for n, (name, src, dst) in enumerate((
            ("vol", vol_in, vol), ("fg", fg_in, fg), ("w1t", w1t_in, w1t), ("w2t", w2t_in, w2t), ("w3t", w3t_in, w3t),
        )):
            loads[name] = pltpu.make_async_copy(src, dst, ls.at[n])
            loads[name].start()

        def loaded(*names):
            for name in names:
                loads.pop(name).wait()

        more_x = jnp.where(s == ns - 1, 0.0, 1.0).astype(F32)
        more_y = jnp.where(y == ny - 1, 0.0, 1.0).astype(F32)
        less_x = jnp.where(s == 0, 0.0, 1.0).astype(F32)
        less_y = jnp.where(y == 0, 0.0, 1.0).astype(F32)
        more_xy = more_x * more_y

        row, lane = grid(80, 256)
        edge = marks(
            ((row < 32) & (lane == (row >> 3) * 64 + (row & 7)))
            | ((row >= 32) & (row < 64) & (lane == (row - 32) * 8))
            | ((row >= 64) & (row < 68) & (lane == (row - 64) * 64))
        )
        for ref, last in ((s1, 127), (s2, 63), (s3, 31)):
            row, lane = grid(256, 128)
            for f in range(3):
                hit = row == 2 * lane + f
                if f == 2:
                    hit = hit & ((lane & last) != last)
                ref[:, f * 128:(f + 1) * 128] = marks(hit)
        row, lane = grid(128, 96)
        pm[...] = marks(((row & 15) == (lane >> 3)) & ((row >> 4) == (lane & 7)))

        loaded("vol", "fg")
        for b in range(4):
            hs[b] = mm(edge, vol[b]).astype(BF16)
        fgs[y] = fg[...]
        pl.semaphore_wait(barrier, len(greeted))
        vol_row = send(hs.at[:, pl.ds(32, 32)], hr.at[:, pl.ds(32, 32)], prev[1])
        vol_plane = send(hs.at[:, pl.ds(0, 32)], hr.at[:, pl.ds(0, 32)], prev[0])
        vol_corner = send(hs.at[:, pl.ds(64, 16)], hr.at[:, pl.ds(64, 16)], prev[2])

        for b in range(4):
            part = mm(vol[b], s1[...]).reshape(4, 8, 8, 384)
            for x in range(8):
                rows = part[:, x].reshape(32, 384)
                rows = jnp.concatenate([rows[:, f * 128:(f + 1) * 128] for f in range(3)], axis=0)
                vsm[x, :, b * 128:(b + 1) * 128] = rows.astype(BF16)
        for x in range(8):
            e1[x, 0:8] = mm(pm[...], vsm[x]).astype(BF16).reshape(8, 16, 512)
        loaded("w1t", "w2t", "w3t")
        row, lane = grid(144, 108)
        pads = marks((lane == (row >> 4) * 12 + (row & 15)) & ((row & 15) < 12))
        w1rows = w1t[...].astype(F32).reshape(108, 16).astype(BF16)
        w1[...] = mm_t(identity(16), mm(pads, w1rows).astype(BF16)).astype(BF16)
        w2[...] = mm_t(identity(32), w2t[...]).astype(BF16)

        def columns_one(i, j):
            return jnp.concatenate(
                [e1[2 * i + a, 2 * j:2 * j + 3].reshape(48, 512) for a in range(3)], axis=0
            )

        def cell_one(i, j):
            act, slope = activate(mm(w1[...], columns_one(i, j)))
            a1[i, j] = act
            sl1[i * 4 + j] = slope

        def widen_two(cells, keep=None):
            rows = jnp.concatenate([a1[i, j] for i, j in cells], axis=0)
            rows = jnp.concatenate([rows[:, :256], rows[:, 256:]], axis=0)
            part = mm(rows, s2[...])
            if keep is not None:
                part = part * keep
            part = part.astype(BF16).reshape(2, len(cells), 16, 384)
            for p in range(2):
                for n, (i, j) in enumerate(cells):
                    for f in range(3):
                        e2[i, j, f * 16:(f + 1) * 16, p * 128:(p + 1) * 128] = (
                            part[p, n, :, f * 128:(f + 1) * 128]
                        )

        def columns_two(i, j):
            return jnp.concatenate(
                [e2[2 * i + a, 2 * j:2 * j + 3].reshape(144, 256) for a in range(3)], axis=0
            )

        def cell_two(i, j):
            act, slope = activate(mm(w2[...], columns_two(i, j)))
            a2[i, j] = act
            sl2[i + 1, j + 1] = slope

        def widen_three(cells, keep=None):
            part = mm(jnp.concatenate([a2[i, j] for i, j in cells], axis=0), s3[...])
            if keep is not None:
                part = part * keep
            part = part.astype(BF16).reshape(len(cells), 32, 384)
            for n, (i, j) in enumerate(cells):
                for f in range(3):
                    e3[i, j, f * 32:(f + 1) * 32, :] = part[n, :, f * 128:(f + 1) * 128]

        for i in range(3):
            cell_one(i, 0)
        act_row = send(a1.at[pl.ds(0, 3), 0], a1.at[pl.ds(0, 3), 4], prev[1])
        for j in range(1, 3):
            cell_one(0, j)
        act_plane = send(a1.at[0, pl.ds(0, 3)], a1.at[4, pl.ds(0, 3)], prev[0])
        act_corner = send(a1.at[0, 0], a1.at[4, 4], prev[2])
        for i in range(1, 3):
            for j in range(1, 3):
                cell_one(i, j)
        widen_two([(i, j) for i in range(3) for j in range(3)])
        cell_two(0, 0)
        two_row = send(a2.at[0, 0], a2.at[0, 2], prev[1])
        two_plane = send(a2.at[0, 0], a2.at[2, 0], prev[0])
        two_corner = send(a2.at[0, 0], a2.at[2, 2], prev[2])
        got_fg = send_all([(fgs.at[y], fgs.at[y], device) for device in y_peers], fgs.at[pl.ds(0, ny - 1)])
        widen_three([(0, 0)])

        w3[...] = mm_t(identity(64), w3t[...]).astype(BF16)
        w2rows = w2t[...].reshape(9, 3, 16, 32)
        w3rows = w3t[...].reshape(9, 3, 32, 64)
        for f in range(3):
            w2k[:, f * 32:(f + 1) * 32] = w2rows[:, f].reshape(144, 32)
            w3k[:, f * 64:(f + 1) * 64] = w3rows[:, f].reshape(288, 64)
        row, lane = grid(512, 128)
        regroup = marks(row == (lane >> 5) * 128 + y * 32 + (lane & 31))

        def widen_volume(at, keep):
            part = mm(hr[:, at:at + 32].reshape(128, 256), s1[...]) * keep
            rows = jnp.concatenate(
                [
                    jnp.concatenate(
                        [part[b * 32:(b + 1) * 32, f * 128:(f + 1) * 128] for f in range(3)], axis=0
                    )
                    for b in range(4)
                ],
                axis=1,
            )
            return mm(pm[...], rows.astype(BF16)).astype(BF16).reshape(8, 16, 512)

        arrive(vol_plane)
        e1[8, 0:8] = widen_volume(0, more_x)
        cell_one(3, 0)
        act_row_end = send(a1.at[3, 0], a1.at[3, 4], prev[1])
        arrive(vol_row)
        block = widen_volume(32, more_y)
        for x in range(8):
            e1[x, 8] = block[x]
        cell_one(0, 3)
        act_plane_end = send(a1.at[0, 3], a1.at[4, 3], prev[0])
        for n in range(1, 3):
            cell_one(n, 3)
            cell_one(3, n)
        widen_two([(3, 0), (3, 1), (3, 2)])
        arrive(act_plane)
        widen_two([(4, 0), (4, 1), (4, 2)], more_x)
        cell_two(1, 0)
        two_row_end = send(a2.at[1, 0], a2.at[1, 2], prev[1])
        widen_two([(0, 3), (1, 3), (2, 3)])
        arrive(act_row)
        widen_two([(0, 4), (1, 4), (2, 4)], more_y)
        cell_two(0, 1)
        two_plane_end = send(a2.at[0, 1], a2.at[2, 1], prev[0])
        widen_three([(0, 1), (1, 0)])
        arrive_all(got_fg)
        cotangent = mm(jnp.concatenate([fgs[k] for k in range(4)], axis=1), regroup)
        arrive(vol_corner)
        part = mm(hr[:, 64:80].reshape(64, 256), s1[...]) * more_xy
        rows = jnp.concatenate(
            [
                jnp.concatenate(
                    [part[b * 16:(b + 1) * 16, f * 128:(f + 1) * 128] for f in range(3)], axis=0
                )
                for b in range(4)
            ],
            axis=1,
        )
        row, lane = grid(16, 48)
        picked = marks((row == (lane >> 4) * 4 + (lane & 15)) & ((lane & 15) < 4))
        e1[8, 8] = mm(picked, rows.astype(BF16)).astype(BF16)
        cell_one(3, 3)
        widen_two([(3, 3)])
        arrive(act_corner)
        widen_two([(4, 4)], more_xy)
        arrive(act_plane_end)
        widen_two([(4, 3)], more_x)
        arrive(act_row_end)
        widen_two([(3, 4)], more_y)
        cell_two(1, 1)
        got_slope = [
            send(sl2.at[2, pl.ds(1, 2)], sl2.at[0, pl.ds(1, 2)], following[0]),
            send(sl2.at[pl.ds(1, 2), 2], sl2.at[pl.ds(1, 2), 0], following[1]),
            send(sl2.at[2, 2], sl2.at[0, 0], following[2]),
        ]
        widen_three([(1, 1)])
        arrive(two_row, two_row_end)
        widen_three([(0, 2), (1, 2)], more_y)
        arrive(two_plane, two_plane_end)
        widen_three([(2, 0), (2, 1)], more_x)
        arrive(two_corner)
        widen_three([(2, 2)], more_xy)

        columns_three = e3[...].reshape(864, 128)
        act, slope = activate(mm(w3[...], columns_three))
        grad_three = (cotangent * slope.astype(F32)).astype(BF16)
        g3[3] = grad_three
        got_grad = [send(g3.at[3], g3.at[to], following[i]) for i, to in ((2, 0), (1, 2), (0, 1))]

        part = mm_t(columns_three, grad_three)
        part = jnp.concatenate([part[:432], part[432:]], axis=1).astype(BF16)
        wb3[...] = jnp.zeros_like(wb3)
        for n in range(27):
            group, at = divmod(n * 16, rows3)
            wb3[group, at:at + 16] = part[n * 16:(n + 1) * 16]
        got_r3 = send_all([(wb3.at[m], r3.at[d], near[d]) for d, m in enumerate(near_ids)], r3)
        fts[y] = act
        got_feat = send_all([(fts.at[y], fts.at[y], device) for device in y_peers], fts.at[pl.ds(0, ny - 1)])

        arrive(*got_grad)
        row, lane = grid(256, 128)
        inside = jnp.where(
            row < 64, less_x * less_y, jnp.where(row < 128, less_x, jnp.where(row < 192, less_y, 1.0))
        )
        rows = (g3[...].reshape(256, 128).astype(F32) * inside).astype(BF16)
        for f in range(3):
            part = mm_t(rows, s3[:, f * 128:(f + 1) * 128]).astype(BF16)
            gg3[:, f * 64:(f + 1) * 64, :] = part.reshape(4, 64, 256)

        def spread(taps, weights, widened, width, channels):
            down = {}
            for i in taps:
                for j in taps:
                    pairs = [(a, e) for a in taps[i] for e in taps[j]]
                    picked = jnp.concatenate(
                        [weights[(a * 3 + e) * channels:(a * 3 + e + 1) * channels, :] for a, e in pairs], axis=0
                    )
                    part = mm(picked, widened[(i + 1) * width + j + 1])
                    for n, (a, e) in enumerate(pairs):
                        key = (2 * i + a, 2 * j + e)
                        term = part[n * channels:(n + 1) * channels]
                        down[key] = term if key not in down else down[key] + term
            return down

        down = spread(TAPS_THREE, w3k, gg3, 2, 32)
        arrive(*got_slope)
        for i in range(-1, 2):
            for j in range(-1, 2):
                rounded = down[i, j].astype(BF16).astype(F32)
                g2e[(i + 1) * 3 + j + 1] = (rounded * sl2[i + 1, j + 1].astype(F32)).astype(BF16)

        part = None
        for i in range(2):
            for j in range(2):
                term = mm_t(columns_two(i, j), g2e[(i + 1) * 3 + j + 1])
                part = term if part is None else part + term
        wb2[...] = jnp.zeros_like(wb2)
        for n in range(432 // rows2):
            lanes, at = divmod(n * rows2, 112)
            wb2[at // rows2, :, lanes * 32:(lanes + 1) * 32] = part[n * rows2:(n + 1) * rows2]
        got_r2 = send_all([(wb2.at[m], r2.at[d], near[d]) for d, m in enumerate(near_ids)], r2)

        for p in range(2):
            rows = g2e[...].reshape(288, 256)[:, p * 128:(p + 1) * 128]
            for f in range(3):
                part = mm_t(rows, s2[:, f * 128:(f + 1) * 128]).astype(BF16)
                gg2[:, f * 32:(f + 1) * 32, p * 256:(p + 1) * 256] = part.reshape(9, 32, 256)
        down = spread(TAPS_TWO, w2k, gg2, 3, 16)

        part = None
        for i in range(4):
            for j in range(4):
                d1b[(i * 4 + j) * 16:(i * 4 + j + 1) * 16, :] = down[i, j].astype(BF16)
                grad_one = (down[i, j] * sl1[i * 4 + j].astype(F32)).astype(BF16)
                term = mm_t(columns_one(i, j), grad_one)
                part = term if part is None else part + term
        part = jnp.concatenate([part[t * 16:t * 16 + 12] for t in range(9)] + [jnp.zeros((20, 16), F32)], axis=0)
        y1[near_me] = part.T.astype(BF16)
        got_y1 = send_all([(y1.at[near_me], y1.at[near_me], device) for device in near], y1.at[pl.ds(0, n_near - 1)])

        def total(first, refs):
            value = first.astype(F32)
            for ref in refs:
                value = value + ref.astype(F32)
            return value

        arrive_all(got_r3)
        z3[far_me] = total(wb3[near_me], [r3[d] for d in range(n_near - 1)])
        got_z3 = send_all([(z3.at[far_me], z3.at[far_me], device) for device in far], z3.at[pl.ds(0, n_far - 1)])
        row, lane = grid(256, 256)
        swap = marks(((row >> 4) == (lane & 15)) & ((row & 15) == (lane >> 4)))
        block = mm(swap, d1b[...]).astype(BF16)
        for b in range(4):
            gact[b] = block[:, b * 128:(b + 1) * 128]
        store(gact, gact_out)
        arrive_all(got_feat)
        feat[...] = mm(jnp.concatenate([fts[k] for k in range(4)], axis=1), regroup).astype(BF16)
        store(feat, feat_out)
        arrive_all(got_r2)
        z2[far_me] = total(wb2[near_me], [r2[d] for d in range(n_near - 1)])
        got_z2 = send_all([(z2.at[far_me], z2.at[far_me], device) for device in far], z2.at[pl.ds(0, n_far - 1)])
        arrive_all(got_y1)
        z1[far_me] = total(y1[0], [y1[m] for m in range(1, n_near)])
        got_z1 = send_all([(z1.at[far_me], z1.at[far_me], device) for device in far], z1.at[pl.ds(0, n_far - 1)])

        arrive_all(got_z3)
        f3[near_me] = (total(z3[0], [z3[m] for m in range(1, n_far)]) * scales[2]).astype(BF16)
        got_f3 = send_all([(f3.at[near_me], f3.at[near_me], device) for device in near], f3.at[pl.ds(0, n_near - 1)])
        arrive_all(got_z2)
        f2[near_me] = total(z2[0], [z2[m] for m in range(1, n_far)]) * scales[1]
        got_f2 = send_all([(f2.at[near_me], f2.at[near_me], device) for device in near], f2.at[pl.ds(0, n_near - 1)])
        arrive_all(got_z1)
        part = total(z1[0], [z1[m] for m in range(1, n_far)]) * scales[0]
        o1[...] = part.T[:108].reshape(27, 4, 16)
        store(o1, o1_out)
        arrive_all(got_f3)
        store(f3, o3_out)
        arrive_all(got_f2)
        store(f2, o2_out)
        for copy in started:
            copy.wait_send()
        for landed, n in grouped:
            pltpu.make_async_copy(landed, landed, ss.at[n]).wait()
        for copy in stores:
            copy.wait()

    vm = pltpu.VMEM
    scratch = [
        vm((4, 256, 256), BF16), vm((27, 4, 16), BF16), vm((432, 32), BF16), vm((864, 64), BF16), vm((64, 128), BF16),
        pltpu.SemaphoreType.DMA((5,)),
        vm((64, 128), BF16), vm((4, 256, 128), BF16), vm((27, 4, 16), F32),
        pltpu.SemaphoreType.DMA((5,)),
        vm((256, 384), BF16), vm((256, 384), BF16), vm((256, 384), BF16), vm((128, 96), BF16),
        vm((16, 144), BF16), vm((32, 432), BF16), vm((64, 864), BF16), vm((144, 96), BF16), vm((288, 192), BF16),
        vm((4, 80, 256), BF16), vm((4, 80, 256), BF16), vm((8, 96, 512), BF16),
        vm((9, 9, 16, 512), BF16), vm((5, 5, 16, 512), BF16), vm((16, 16, 512), BF16), vm((5, 5, 48, 256), BF16),
        vm((3, 3, 32, 256), BF16), vm((3, 3, 32, 256), BF16), vm((3, 3, 96, 128), BF16),
        vm((4, 64, 128), BF16), vm((4, 64, 128), BF16), vm((4, 64, 128), BF16), vm((4, 192, 256), BF16),
        vm((9, 32, 256), BF16), vm((9, 96, 512), BF16), vm((256, 512), BF16),
        vm((n_near, rows3, 128), BF16), vm((n_near - 1, rows3, 128), BF16), vm((n_far, rows3, 128), F32),
        vm((n_near, rows3, 128), BF16),
        vm((n_near, rows2, 128), F32), vm((n_near - 1, rows2, 128), F32), vm((n_far, rows2, 128), F32),
        vm((n_near, rows2, 128), F32),
        vm((n_near, 16, 128), BF16), vm((n_far, 16, 128), F32),
        pltpu.SemaphoreType.DMA((COPIES,)), pltpu.SemaphoreType.DMA((COPIES,)),
    ]
    return pl.pallas_call(
        kernel,
        out_shape=(
            jax.ShapeDtypeStruct((64, 128), BF16),
            jax.ShapeDtypeStruct((4, 256, 128), BF16),
            jax.ShapeDtypeStruct((27, 4, 16), F32),
            jax.ShapeDtypeStruct((n_near, rows2, 128), F32),
            jax.ShapeDtypeStruct((n_near, rows3, 128), BF16),
        ),
        in_specs=[pl.BlockSpec(memory_space=pltpu.HBM)] * 5,
        out_specs=[pl.BlockSpec(memory_space=pltpu.HBM)] * 5,
        scratch_shapes=scratch,
        compiler_params=pltpu.CompilerParams(
            collective_id=0, has_side_effects=True, vmem_limit_bytes=60 * 1024 * 1024
        ),
        cost_estimate=pl.CostEstimate(flops=3_000_000_000, bytes_accessed=4_000_000, transcendentals=0),
        name="layers",
    )


def hand_over(*refs):
    given, results, held = refs[:5], refs[5:10], refs[10:15]
    two, three, sems = refs[15:]
    parts = [(4, None), (3, None), (2, None), (0, None)] + [(1, b) for b in range(4)]

    def part(ref, b):
        return ref if b is None else ref.at[b]

    come = [
        pltpu.make_async_copy(part(given[n], b), part(held[n], b), sems.at[k]) for k, (n, b) in enumerate(parts)
    ]
    source = {0: held[0], 1: held[1], 2: held[2], 3: two, 4: three}
    go = [
        pltpu.make_async_copy(part(source[n], b), part(results[n], b), sems.at[8 + k])
        for k, (n, b) in enumerate(parts)
    ]
    for copy in come:
        copy.start()
    for k in range(2, 8):
        come[k].wait()
        go[k].start()
    come[0].wait()
    packed = held[4][...].astype(F32).reshape(512, 128)[:432]
    for half in range(2):
        three[half * 432:(half + 1) * 432, :] = packed[:, half * 64:(half + 1) * 64]
    go[0].start()
    come[1].wait()
    packed = held[3][...].reshape(128, 128)
    for n in range(27):
        lanes, at = divmod(n * 16, 112)
        two[n * 16:(n + 1) * 16, :] = packed[at:at + 16, lanes * 32:(lanes + 1) * 32]
    go[1].start()
    for copy in go:
        copy.wait()


def solution(mesh):
    ny, ns = mesh.shape["sample"], mesh.shape["space"]
    nx = 4 if ns % 8 == 0 else 1

    def local(volumes, weight_one, weight_two, weight_three, feature_grad):
        cells = volumes.shape[0] * volumes.shape[2] * ns * volumes.shape[3] * ny * volumes.shape[4]
        scales = [GRAD_GAIN / math.sqrt(cells // 8**n) for n in (1, 2, 3)]
        flat = [
            jnp.transpose(w, (2, 3, 4, 1, 0)).reshape(shape)
            for w, shape in ((weight_one, (27, 4, 16)), (weight_two, (432, 32)), (weight_three, (864, 64)))
        ]
        features, grad_act, one, two, three = make_kernel(ny, ns, nx, scales)(
            volumes.reshape(4, 256, 256), *flat, feature_grad.reshape(64, 128)
        )

        features, grad_act, one, two, three = pl.pallas_call(
            hand_over,
            out_shape=(
                jax.ShapeDtypeStruct((64, 128), BF16),
                jax.ShapeDtypeStruct((4, 256, 128), BF16),
                jax.ShapeDtypeStruct((27, 4, 16), F32),
                jax.ShapeDtypeStruct((432, 32), F32),
                jax.ShapeDtypeStruct((864, 64), F32),
            ),
            in_specs=[pl.BlockSpec(memory_space=pltpu.HBM)] * 5,
            out_specs=[pl.BlockSpec(memory_space=pltpu.HBM)] * 5,
            scratch_shapes=[
                pltpu.VMEM((64, 128), BF16), pltpu.VMEM((4, 256, 128), BF16), pltpu.VMEM((27, 4, 16), F32),
                pltpu.VMEM(two.shape, F32), pltpu.VMEM(three.shape, BF16),
                pltpu.VMEM((432, 32), F32), pltpu.VMEM((864, 64), F32), pltpu.SemaphoreType.DMA((16,)),
            ],
            compiler_params=pltpu.CompilerParams(vmem_limit_bytes=63 * 1024 * 1024),
            name="hand_over",
        )(features, grad_act, one, two, three)

        def filters(array, channels):
            return jnp.transpose(array.reshape(3, 3, 3, channels, -1), (4, 3, 0, 1, 2))

        return (
            features.reshape(feature_grad.shape),
            grad_act.reshape(4, 16, 4, 4, 128),
            filters(one, 4),
            filters(two, 16),
            filters(three, 32),
        )

    in_specs = (
        P(None, None, "space", "sample", None),
        P(),
        P(),
        P(),
        P("sample", None, "space", None),
    )
    out_specs = (
        P("sample", None, "space", None),
        P(None, None, "space", "sample", None),
        P(),
        P(),
        P(),
    )
    return jax.shard_map(local, mesh=mesh, in_specs=in_specs, out_specs=out_specs, check_vma=False)
```
